32 devices in a mesh: groups: 2 (over x), fsdp: 8 (over z, y), tp: 2 (over core).
Axes of the slice: x: 2, y: 2, z: 4, core: 2. Of those that a mesh axis runs over, the one named last changes fastest.
Arguments:
- queries: bfloat16 [64, 4, 128, 128], P(('groups', 'fsdp'), None, 'tp'), parts along dimension 0, may hold values from -128 to 128
- cache_keys: bfloat16 [64, 512, 8, 128], P(('groups', 'fsdp'), None, 'tp'), parts along dimension 0, may hold values from -6 to 6
- cache_values: bfloat16 [64, 512, 8, 128], P(('groups', 'fsdp'), None, 'tp'), parts along dimension 0, may hold values from -6 to 6
- new_keys: bfloat16 [64, 4, 8, 128], P(('groups', 'fsdp'), None, 'tp'), parts along dimension 0, may hold values from -12 to 12
- new_values: bfloat16 [64, 4, 8, 128], P(('groups', 'fsdp'), None, 'tp'), parts along dimension 0, may hold values from -6 to 6
- cache_lengths: int32 [64], P(('groups', 'fsdp')), parts along dimension 0, may hold values from 1 to 512, as said below
- base_weight: bfloat16 [16384, 16384], P('tp', 'fsdp'), may hold values from -0.046875 to 0.046875
- factor_in: bfloat16 [32768, 128], P(('groups', 'fsdp'), 'tp'), parts along dimension 0, may hold values from -0.046875 to 0.046875
- adapter_output_factor: bfloat16 [256, 16384], P(('groups', 'tp'), 'fsdp'), parts along dimension 0, may hold values from -0.5 to 0.5
Outputs:
- projected: bfloat16 [64, 4, 16384], P(('groups', 'fsdp'), None, 'tp'), parts along dimension 0
The draws below stay inside these ranges and needn't reach their ends.
There are 2 independent parts, one for each index of `groups`. The reference program is written for one: setup_inputs(seed, part) draws one part's arguments, and reference() takes and returns one part's arrays. A program takes and returns all parts, laid end to end along the dimension named above; an argument that names none is the same for every part. Nothing has to cross between parts.
Inputs may be any that keep to these rules, and one draw needn't show every extreme that they name: The first cache_lengths[r] slots of sequence r are valid; some sequence has all 512.
All inputs are finite; a program needn't handle non-finite values.
Results may differ from the reference program's by a relative error of at most 0.0059.
Values may be sent and summed in bfloat16 or wider, within the bound.
No kernel may reach another device: no remote copies, remote signals or barrier semaphores. Data moves between devices by JAX's collectives and lax.ppermute only.
A program may use at most 128 MiB of HBM per device.

```python
import math
import jax
import jax.numpy as jnp
from jax import lax

D = 16384
HEADS = 128
KV = 8
HD = 128
RANK = 128
LEN = 512
STEPS = 4
IN = 16384
ROWS = 32


def paired(key, lift):
    key_shape = (ROWS, STEPS, KV, HD)
    base_keys = 1.5 * jax.random.truncated_normal(jax.random.fold_in(key, 21), -6.0, 6.0, key_shape, jnp.float32)
    jitter = 0.15 * jax.random.truncated_normal(jax.random.fold_in(key, 22), -6.0, 6.0, key_shape, jnp.float32)
    chosen = (jax.random.uniform(jax.random.fold_in(key, 23), (ROWS, STEPS, KV), jnp.float32) < 0.05).astype(jnp.float32)
    chosen = chosen * (jnp.arange(STEPS) >= 1).astype(jnp.float32)[None, :, None] * lift
    following = jnp.concatenate([chosen[:, 1:], jnp.zeros_like(chosen[:, :1])], 1)
    next_keys = jnp.concatenate([base_keys[:, 1:], base_keys[:, -1:]], 1)
    fresh_keys = base_keys + following[..., None] * (next_keys + jitter - base_keys)
    strength = jax.random.uniform(jax.random.fold_in(key, 24), (ROWS, STEPS, KV, HEADS // KV), jnp.float32, 4.0, 12.0)
    entries = 2.0 * jax.random.truncated_normal(jax.random.fold_in(key, 25), -6.0, 6.0, (ROWS, STEPS, KV, HEADS // KV, HD), jnp.float32)
    aligned = strength[..., None] * fresh_keys[:, :, :, None, :]
    query_all = jnp.where(chosen[..., None, None] > 0.5, aligned, entries).reshape(ROWS, STEPS, HEADS, HD)
    return (query_all, fresh_keys)


def draw_queries(key, part):
    lift = 0.0
    query_all, fresh_keys = paired(key, lift)
    return query_all.astype(jnp.bfloat16)


def draw_new_keys(key, part):
    lift = 0.0
    query_all, fresh_keys = paired(key, lift)
    return fresh_keys.astype(jnp.bfloat16)


def draw_cache_lengths(key, part):
    key = jax.random.fold_in(key, 5)
    drawn = jax.random.randint(jax.random.fold_in(key, 1), (ROWS,), 1, LEN + 1, jnp.int32)
    longest = jax.random.randint(jax.random.fold_in(key, 2), (), 0, ROWS, jnp.int32)
    return jnp.where(jnp.arange(ROWS, dtype=jnp.int32) == longest, LEN, drawn).astype(jnp.int32)


def block_levels(key, dims, split, low, largest):
    gain = 1.0
    for dim, blocks in split:
        heights = jax.random.uniform(jax.random.fold_in(jax.random.fold_in(key, 6), dim), (blocks,), jnp.float32, low / len(split), largest / len(split))
        gain = gain * jnp.repeat(jnp.exp(heights), dims[dim] // blocks).reshape((-1,) + (1,) * (len(dims) - 1 - dim))
    return gain


def noise(rng, extent, width, reach, split=(), kind=jnp.bfloat16):
    result = jax.random.normal(rng, extent, jnp.float32) * width
    if len(split) > 0:
        result = block_levels(rng, extent, split, -0.22, 0.18) * result
    return jnp.clip(result, min=-reach, max=reach).astype(kind)


def setup_inputs(seed: int = 0, part: int = 0) -> dict:
    splits = jax.random.split(jax.random.key(seed), 10)
    own_keys = jax.random.split(jax.random.fold_in(splits[9], part), 10)
    queries = draw_queries(jax.random.fold_in(jax.random.fold_in(splits[9], part), 71), part)
    cache_keys = noise(own_keys[1], (ROWS, LEN, KV, HD), 1.0, 6.0, ((0, 8), (2, 2)))
    cache_values = noise(own_keys[2], (ROWS, LEN, KV, HD), 1.0, 6.0, ((0, 8), (2, 2)))
    new_keys = draw_new_keys(jax.random.fold_in(jax.random.fold_in(splits[9], part), 71), part)
    new_values = noise(own_keys[4], (ROWS, STEPS, KV, HD), 1.0, 6.0, ((0, 8), (2, 2)))
    cache_lengths = draw_cache_lengths(jax.random.fold_in(jax.random.fold_in(splits[9], part), 71), part)
    base_weight = noise(splits[6], (IN, D), IN ** -0.5, 0.046875, ((0, 2), (1, 8)))
    factor_in = noise(own_keys[7], (IN, RANK), IN ** -0.5, 0.046875, ((0, 8), (1, 2)))
    adapter_output_factor = noise(own_keys[8], (RANK, D), RANK ** -0.5, 0.5, ((0, 2), (1, 8)))
    return {"queries": queries, "cache_keys": cache_keys, "cache_values": cache_values, "new_keys": new_keys, "new_values": new_values, "cache_lengths": cache_lengths, "base_weight": base_weight, "factor_in": factor_in, "adapter_output_factor": adapter_output_factor}


adapter_scale = 2.0

def attend_row(inputs):
    query_now, keys_old, values_old, keys_fresh, values_fresh, valid_count = inputs
    step_count, head_count, head_width = query_now.shape
    key_heads = keys_old.shape[1]
    query_now = query_now.astype(jnp.float32).reshape(step_count, key_heads, head_count // key_heads, head_width)
    score_scale = 1.0 / math.sqrt(head_width)
    old_scores = jnp.einsum('sgqd,lgd->gsql', query_now, keys_old.astype(jnp.float32)) * score_scale
    visible = jnp.arange(keys_old.shape[0], dtype=jnp.int32) < valid_count
    old_scores = jnp.where(visible, old_scores, -jnp.inf)
    new_scores = jnp.einsum('sgqd,tgd->gsqt', query_now, keys_fresh.astype(jnp.float32)) * score_scale
    causal = jnp.arange(step_count)[None, :] <= jnp.arange(step_count)[:, None]
    new_scores = jnp.where(causal[None, :, None, :], new_scores, -jnp.inf)
    highest = jnp.maximum(old_scores.max(-1), new_scores.max(-1))
    old_weights = jnp.exp(old_scores - highest[..., None])
    new_weights = jnp.exp(new_scores - highest[..., None])
    totals = old_weights.sum(-1) + new_weights.sum(-1)
    old_probs = lax.optimization_barrier(old_weights.astype(jnp.bfloat16)).astype(jnp.float32)
    new_probs = lax.optimization_barrier(new_weights.astype(jnp.bfloat16)).astype(jnp.float32)
    weighted = jnp.einsum('gsql,lgd->sgqd', old_probs, values_old.astype(jnp.float32))
    weighted = weighted + jnp.einsum('gsqt,tgd->sgqd', new_probs, values_fresh.astype(jnp.float32))
    attended = weighted / jnp.transpose(totals, (1, 0, 2))[..., None]
    return attended.astype(jnp.bfloat16).reshape(step_count, head_count * head_width)

def reference(queries, cache_keys, cache_values, new_keys, new_values, cache_lengths, base_weight, factor_in, adapter_output_factor):
    attended = lax.map(attend_row, (queries, cache_keys, cache_values, new_keys, new_values, cache_lengths))
    flattened = attended.reshape(ROWS * STEPS, IN)
    block_rows = math.gcd(IN, 1024)

    def add_block(running, position):
        offset = (position * block_rows).astype(jnp.int32)
        frozen_weight_rows = lax.dynamic_slice_in_dim(base_weight, offset, block_rows, 0)
        adapter_row_count = lax.dynamic_slice_in_dim(factor_in, offset, block_rows, 0)
        combined_weight = (frozen_weight_rows.astype(jnp.float32) + adapter_scale * jnp.dot(adapter_row_count, adapter_output_factor, preferred_element_type=jnp.float32)).astype(jnp.bfloat16)
        columns = lax.dynamic_slice_in_dim(flattened, offset, block_rows, 1)
        return (running + jnp.dot(columns, combined_weight, preferred_element_type=jnp.float32), None)
    start_sum = jnp.zeros((ROWS * STEPS, D), jnp.float32)
    running, _ = lax.scan(add_block, start_sum, jnp.arange(IN // block_rows, dtype=jnp.int32))
    return running.astype(jnp.bfloat16).reshape(ROWS, STEPS, D)
```

```python
import functools
import math

import jax
import jax.numpy as jnp
from jax import lax
from jax.experimental import pallas as pl
from jax.experimental.pallas import tpu as pltpu
from jax.sharding import PartitionSpec as P

adapter_scale = 2.0
chunk_count = 2


def attend(queries, cache_keys, cache_values, new_keys, new_values, cache_lengths):
    row_count, step_count, head_count, head_width = queries.shape
    key_heads = cache_keys.shape[2]
    slot_count = cache_keys.shape[1]
    query_now = queries.reshape(
        row_count, step_count, key_heads, head_count // key_heads, head_width
    )
    score_scale = 1.0 / math.sqrt(head_width)
    old_scores = (
        jnp.einsum("rsgqd,rlgd->rgsql", query_now, cache_keys, preferred_element_type=jnp.float32)
        * score_scale
    )
    visible = jnp.arange(slot_count, dtype=jnp.int32)[None, :] < cache_lengths[:, None]
    old_scores = jnp.where(visible[:, None, None, None, :], old_scores, -jnp.inf)
    new_scores = (
        jnp.einsum("rsgqd,rtgd->rgsqt", query_now, new_keys, preferred_element_type=jnp.float32)
        * score_scale
    )
    steps = jnp.arange(step_count)
    causal = steps[None, :] <= steps[:, None]
    new_scores = jnp.where(causal[None, None, :, None, :], new_scores, -jnp.inf)
    highest = jnp.maximum(old_scores.max(-1), new_scores.max(-1))
    old_weights = jnp.exp(old_scores - highest[..., None])
    new_weights = jnp.exp(new_scores - highest[..., None])
    totals = old_weights.sum(-1) + new_weights.sum(-1)
    weighted = jnp.einsum(
        "rgsql,rlgd->rsgqd",
        old_weights.astype(jnp.bfloat16),
        cache_values,
        preferred_element_type=jnp.float32,
    )
    weighted = weighted + jnp.einsum(
        "rgsqt,rtgd->rsgqd",
        new_weights.astype(jnp.bfloat16),
        new_values,
        preferred_element_type=jnp.float32,
    )
    attended = weighted / jnp.transpose(totals, (0, 2, 1, 3))[..., None]
    return attended.astype(jnp.bfloat16).reshape(row_count * step_count, head_count * head_width)


def ring_order(count):
    inner = max(d for d in range(1, count + 1) if count % d == 0 and d * d <= count)
    outer = count // inner
    if inner == 1:
        return list(range(count))
    order = [z * inner for z in range(outer)]
    for turn, z in enumerate(reversed(range(outer))):
        columns = list(range(1, inner))
        if turn % 2:
            columns.reverse()
        order += [z * inner + c for c in columns]
    return order


def ring_gather(block, order):
    count = len(order)
    up = [(order[i], order[(i + 1) % count]) for i in range(count)]
    down = [(b, a) for a, b in up]
    blocks = {0: block}
    rising = falling = block
    for step in range(1, count // 2):
        rising = lax.ppermute(rising, "fsdp", up)
        falling = lax.ppermute(falling, "fsdp", down)
        blocks[count - step] = rising
        blocks[step] = falling
    half = block.shape[1] // 2
    far_left = lax.ppermute(rising[:, :half], "fsdp", up)
    far_right = lax.ppermute(falling[:, half:], "fsdp", down)
    near = [blocks[i] for i in range(count) if i != count // 2]
    return near, (far_left, far_right)


def project_kernel(count, per_tile, with_previous, *refs):
    places, flags = refs[:2]
    near = refs[2 : count + 1]
    far_left, far_right, weight, own_in, other_in = refs[count + 1 : count + 6]
    rest = refs[count + 6 :]
    if with_previous:
        previous, previous_rank = rest[:2]
        rest = rest[2:]
    partial, ranked, attended, factor = rest
    step = pl.program_id(0)
    half = far_left.shape[1]
    block_rows = far_left.shape[0]
    rank_half, own_width = own_in.shape

    @pl.when(step == 0)
    def _():
        for place, ref in enumerate(near):
            place = place if place < count // 2 else place + 1
            attended[places[place]] = ref[...]
        far = places[count // 2]
        attended[far, :, :half] = far_left[...]
        attended[far, :, half:] = far_right[...]
        if with_previous:
            partial[...] = previous[...]
            ranked[...] = previous_rank[...]
        else:
            partial[...] = jnp.zeros_like(partial)
            ranked[...] = jnp.zeros_like(ranked)

        @pl.when(flags[0] == 1)
        def _():
            core = flags[2]
            factor[pl.ds(pl.multiple_of(core * rank_half, rank_half), rank_half), :] = own_in[...]
            factor[pl.ds(pl.multiple_of((1 - core) * rank_half, rank_half), rank_half), :] = (
                other_in[...]
            )
            columns = pl.ds(pl.multiple_of(flags[1], 128), own_width)
            rows = attended[:, :, columns].reshape(count * block_rows, own_width)
            ranked[...] += lax.dot_general(
                rows, factor[...], (((1,), (1,)), ((), ())), preferred_element_type=jnp.float32
            )

    columns = pl.ds(pl.multiple_of(step * per_tile, per_tile), per_tile)
    rows = attended[:, :, columns].reshape(count * block_rows, per_tile)
    partial[...] += jnp.dot(rows, weight[...], preferred_element_type=jnp.float32)


def project(chunk, places, flags, near, far, base_weight, own_in, other_in, previous):
    count = len(near) + 1
    block_rows, width = near[0].shape
    columns = base_weight.shape[1]
    per_tile = min(width, 1024)
    tiles = width // per_tile
    rows = count * block_rows
    rank = 2 * own_in.shape[0]

    def whole(shape):
        return pl.BlockSpec(shape, lambda *_: (0,) * len(shape))

    operands = [*near, *far, base_weight, own_in, other_in]
    specs = [whole(x.shape) for x in operands]
    specs[len(near) + 2] = pl.BlockSpec(
        (per_tile, columns), lambda k, *_: (chunk * tiles + k, 0)
    )
    if previous is not None:
        operands += list(previous)
        specs += [whole(x.shape) for x in previous]
    return pl.pallas_call(
        functools.partial(project_kernel, count, per_tile, previous is not None),
        grid_spec=pltpu.PrefetchScalarGridSpec(
            num_scalar_prefetch=2,
            grid=(tiles,),
            in_specs=specs,
            out_specs=[whole((rows, columns)), whole((rows, rank))],
            scratch_shapes=[
                pltpu.VMEM((count, block_rows, width), jnp.bfloat16),
                pltpu.VMEM((rank, own_in.shape[1]), jnp.bfloat16),
            ],
        ),
        out_shape=[
            jax.ShapeDtypeStruct((rows, columns), jnp.float32),
            jax.ShapeDtypeStruct((rows, rank), jnp.float32),
        ],
        compiler_params=pltpu.CompilerParams(vmem_limit_bytes=40 * 1024 * 1024),
        cost_estimate=pl.CostEstimate(
            flops=4 * rows * width * columns,
            bytes_accessed=2 * width * columns,
            transcendentals=0,
        ),
        name=f"project_{chunk}",
    )(places, flags, *operands)


def adapter_kernel(flags, partial, ranked, own_out, other_out, keep, send, factor):
    core, kept = flags[2], flags[3]
    rank_half = own_out.shape[0]
    rank = 2 * rank_half
    for part in range(2):
        base = part * rank
        factor[pl.ds(pl.multiple_of(base + core * rank_half, rank_half), rank_half), :] = own_out[...]
        factor[pl.ds(pl.multiple_of(base + (1 - core) * rank_half, rank_half), rank_half), :] = (
            other_out[...]
        )
    scaled = adapter_scale * ranked[...]
    high = scaled.astype(jnp.bfloat16)
    low = (scaled - high.astype(jnp.float32)).astype(jnp.bfloat16)
    added = jnp.dot(
        jnp.concatenate([high, low], axis=1), factor[...], preferred_element_type=jnp.float32
    )
    total = partial[...] + added
    rows = keep.shape[0]
    first, second = total[:rows], total[rows:]
    keep[...] = jnp.where(kept == 0, first, second)
    send[...] = jnp.where(kept == 0, second, first)


def add_adapter(flags, partial, ranked, own_out, other_out):
    rows, columns = partial.shape
    half = jax.ShapeDtypeStruct((rows // 2, columns), jnp.float32)
    vmem = pl.BlockSpec(memory_space=pltpu.VMEM)
    return pl.pallas_call(
        adapter_kernel,
        in_specs=[pl.BlockSpec(memory_space=pltpu.SMEM)] + [vmem] * 4,
        out_specs=[vmem] * 2,
        out_shape=[half, half],
        scratch_shapes=[pltpu.VMEM((4 * own_out.shape[0], columns), jnp.bfloat16)],
        compiler_params=pltpu.CompilerParams(vmem_limit_bytes=40 * 1024 * 1024),
        name="add_adapter",
    )(flags, partial, ranked, own_out, other_out)


def round_kernel(flags, keep, received, *outs):
    mine = flags[4]
    for offset, out in enumerate(outs):
        total = keep[mine ^ offset] + received[mine ^ offset]
        out[...] = total.astype(jnp.bfloat16).reshape(out.shape)


def round_and_split(flags, keep, received, row_count, step_count):
    rows, columns = keep.shape
    block = row_count * step_count
    pieces = rows // block
    vmem = pl.BlockSpec(memory_space=pltpu.VMEM)
    return pl.pallas_call(
        round_kernel,
        in_specs=[pl.BlockSpec(memory_space=pltpu.SMEM)] + [vmem] * 2,
        out_specs=[vmem] * pieces,
        out_shape=[jax.ShapeDtypeStruct((row_count, step_count, columns), jnp.bfloat16)] * pieces,
        compiler_params=pltpu.CompilerParams(vmem_limit_bytes=40 * 1024 * 1024),
        name="round_and_split",
    )(flags, keep.reshape(pieces, block, columns), received.reshape(pieces, block, columns))


def place_kernel(flags, *refs):
    out = refs[-1]
    mine = flags[4]
    for offset, ref in enumerate(refs[:-1]):
        width = ref.shape[2]
        out[:, :, pl.ds(pl.multiple_of((mine ^ offset) * width, width), width)] = ref[...]


def place(flags, pieces):
    row_count, step_count, width = pieces[0].shape
    vmem = pl.BlockSpec(memory_space=pltpu.VMEM)
    return pl.pallas_call(
        place_kernel,
        in_specs=[pl.BlockSpec(memory_space=pltpu.SMEM)] + [vmem] * len(pieces),
        out_specs=vmem,
        out_shape=jax.ShapeDtypeStruct(
            (row_count, step_count, width * len(pieces)), jnp.bfloat16
        ),
        name="place",
    )(flags, *pieces)


def shards(
    count,
    queries,
    cache_keys,
    cache_values,
    new_keys,
    new_values,
    cache_lengths,
    base_weight,
    factor_in,
    adapter_output_factor,
):
    order = ring_order(count)
    position = {f: i for i, f in enumerate(order)}
    half_count = count // 2
    both = ("fsdp", "tp")
    chip = lax.axis_index("fsdp").astype(jnp.int32)
    core = lax.axis_index("tp").astype(jnp.int32)
    side = chip // half_count
    mine = chip % half_count
    table = jnp.array(
        [[order[(position[f] + i) % count] for i in range(count)] for f in range(count)], jnp.int32
    )
    places = lax.dynamic_index_in_dim(table, chip, 0, keepdims=False)
    row_count, step_count = queries.shape[:2]

    factors = jnp.concatenate([factor_in.T, adapter_output_factor], axis=0)
    other = lax.ppermute(factors, "tp", [(0, 1), (1, 0)])
    rank_half = factor_in.shape[1]
    own_in, other_in = factor_in.T, other[:rank_half]
    own_out, other_out = adapter_output_factor, other[rank_half:]

    attended = attend(queries, cache_keys, cache_values, new_keys, new_values, cache_lengths)
    width = attended.shape[1] // chunk_count
    own_width = factor_in.shape[0]
    gathered = [
        ring_gather(attended[:, c * width : (c + 1) * width], order) for c in range(chunk_count)
    ]
    state = None
    for c, (near, far) in enumerate(gathered):
        start = mine * own_width - c * width
        owns = (core == side) & (start >= 0) & (start < width)
        flags = jnp.stack(
            [owns.astype(jnp.int32), jnp.clip(start, 0, width - own_width), core, core ^ side, mine]
        )
        state = project(c, places, flags, near, far, base_weight, own_in, other_in, state)
    partial, ranked = state

    bit = 1
    while bit < count:
        turn = 1 if bit == half_count else 0
        pairs = [
            (2 * f + t, 2 * (f ^ bit) + (t ^ turn)) for f in range(count) for t in range(2)
        ]
        ranked = ranked + lax.ppermute(ranked, both, pairs)
        bit *= 2

    keep, send = add_adapter(flags, partial, ranked, own_out, other_out)
    received = lax.ppermute(send, "tp", [(0, 1), (1, 0)])
    pieces = round_and_split(flags, keep, received, row_count, step_count)
    landed = []
    for offset, piece in enumerate(pieces):
        pairs = [
            (2 * f + t, 2 * (f ^ (t * half_count + offset)) + f // half_count)
            for f in range(count)
            for t in range(2)
        ]
        landed.append(lax.ppermute(piece, both, pairs))
    return place(flags, landed)


def solution(mesh):
    return jax.shard_map(
        functools.partial(shards, mesh.shape["fsdp"]),
        mesh=mesh,
        in_specs=(
            P(("groups", "fsdp"), None, "tp", None),
            P(("groups", "fsdp"), None, "tp", None),
            P(("groups", "fsdp"), None, "tp", None),
            P(("groups", "fsdp"), None, "tp", None),
            P(("groups", "fsdp"), None, "tp", None),
            P(("groups", "fsdp")),
            P("tp", "fsdp"),
            P(("groups", "fsdp"), "tp"),
            P(("groups", "tp"), "fsdp"),
        ),
        out_specs=P(("groups", "fsdp"), None, "tp"),
        check_vma=False,
    )
```

```python
import functools
import math

import jax
import jax.numpy as jnp
import numpy as np
from jax import lax
from jax.experimental import pallas as pl
from jax.experimental.pallas import tpu as pltpu
from jax.sharding import PartitionSpec as P

adapter_scale = 2.0
chunk_count = 2
weight_edges = (0, 2, 5, 8, 12, 15, 16)
mebibyte = 1024 * 1024


def attend_kernel(
    lengths, queries, keys, values, fresh_keys, fresh_values, *refs
):
    outs, refs = refs[:chunk_count], refs[chunk_count:]
    query_held, key_held, value_held, fresh_key_held, fresh_value_held, key_wide, value_wide, gathered, sems = refs
    row_count, step_count, heads, head_width = query_held.shape
    old_rows, new_rows = key_held.shape[1], fresh_key_held.shape[1]
    groups = new_rows // step_count
    per_group = heads // groups
    slots = old_rows // groups
    columns = key_wide.shape[1] // groups
    rows = step_count * per_group
    exponent_scale = math.log2(math.e) / math.sqrt(head_width)

    fresh = [
        pltpu.make_async_copy(fresh_keys, fresh_key_held, sems.at[0]),
        pltpu.make_async_copy(queries, query_held, sems.at[1]),
        pltpu.make_async_copy(fresh_values, fresh_value_held, sems.at[2]),
    ]
    old_keys = [
        pltpu.make_async_copy(keys.at[row], key_held.at[row], sems.at[3 + row])
        for row in range(row_count)
    ]
    old_values = [
        pltpu.make_async_copy(values.at[row], value_held.at[row], sems.at[3 + row_count + row])
        for row in range(row_count)
    ]
    for copy in fresh:
        copy.start()
    for row in range(row_count):
        old_keys[row].start()
        old_values[row].start()
    for copy in fresh:
        copy.wait()

    column = lax.broadcasted_iota(jnp.int32, (step_count, 1, columns), 2)
    step = lax.broadcasted_iota(jnp.int32, (step_count, 1, columns), 0)
    fresh_seen = (column >= slots) & (column - slots <= step)

    def widen(old, new, wide):
        wide[:old_rows] = old.astype(jnp.float32)
        wide[old_rows : old_rows + new_rows] = new.astype(jnp.float32)
        wide[old_rows + new_rows :] = jnp.zeros_like(wide[old_rows + new_rows :])

    def picked(group):
        return pl.ds(group, columns, stride=groups)

    for row in range(row_count):
        old_keys[row].wait()
        widen(key_held[row], fresh_key_held[row], key_wide.at[row])
        bias = jnp.where((column < jnp.minimum(lengths[row], slots)) | fresh_seen, 0.0, -jnp.inf)
        scores = [
            lax.dot_general(
                query_held[row, :, group * per_group : (group + 1) * per_group, :].reshape(
                    rows, head_width
                ),
                key_wide[row, picked(group), :].astype(jnp.bfloat16),
                (((1,), (1,)), ((), ())),
                preferred_element_type=jnp.float32,
            ).reshape(step_count, per_group, columns)
            + bias
            for group in range(groups)
        ]
        old_values[row].wait()
        widen(value_held[row], fresh_value_held[row], value_wide.at[row])
        tops = [score.max(-1, keepdims=True) for score in scores]
        scores = [
            jnp.exp2((score - top) * exponent_scale) for score, top in zip(scores, tops)
        ]
        totals = [score.sum(-1, keepdims=True) for score in scores]
        weighted = [
            jnp.dot(
                score.astype(jnp.bfloat16).reshape(rows, columns),
                value_wide[row, picked(group), :].astype(jnp.bfloat16),
                preferred_element_type=jnp.float32,
            ).reshape(step_count, per_group, head_width)
            for group, score in enumerate(scores)
        ]
        for group in range(groups):
            result = weighted[group] / totals[group]
            for s in range(step_count):
                place = (row * step_count + s) * heads + group * per_group
                gathered[place : place + per_group, :] = result[s]
    each = heads // chunk_count
    for head in range(heads):
        place = head % each * head_width
        outs[head // each][:, place : place + head_width] = gathered[
            pl.ds(head, row_count * step_count, stride=heads), :
        ].astype(jnp.bfloat16)


def attend(lengths, queries, keys, values, fresh_keys, fresh_values):
    row_count, step_count, heads, head_width = queries.shape
    smem = pl.BlockSpec(memory_space=pltpu.SMEM)
    vmem = pl.BlockSpec(memory_space=pltpu.VMEM)
    anywhere = pl.BlockSpec(memory_space=pl.ANY)
    kind = jnp.bfloat16
    shape = (row_count * step_count, heads * head_width // chunk_count)
    groups = fresh_keys.shape[1] // step_count
    columns = -(-(keys.shape[1] + fresh_keys.shape[1]) // (16 * groups)) * 16
    wide = pltpu.VMEM((row_count, columns * groups, head_width), jnp.float32)
    return pl.pallas_call(
        attend_kernel,
        in_specs=[smem] + [anywhere] * 5,
        out_specs=[vmem] * chunk_count,
        out_shape=[jax.ShapeDtypeStruct(shape, kind)] * chunk_count,
        scratch_shapes=[
            pltpu.VMEM(queries.shape, kind),
            pltpu.VMEM(keys.shape, kind),
            pltpu.VMEM(values.shape, kind),
            pltpu.VMEM(fresh_keys.shape, kind),
            pltpu.VMEM(fresh_values.shape, kind),
            wide,
            wide,
            pltpu.VMEM((row_count * step_count * heads, head_width), jnp.float32),
            pltpu.SemaphoreType.DMA((3 + 2 * row_count,)),
        ],
        compiler_params=pltpu.CompilerParams(vmem_limit_bytes=58 * mebibyte),
        cost_estimate=pl.CostEstimate(
            flops=4 * row_count * step_count * heads * keys.shape[1] * head_width,
            bytes_accessed=4 * keys.size,
            transcendentals=row_count * step_count * heads * keys.shape[1],
        ),
        name="attend",
    )(lengths, queries, keys, values, fresh_keys, fresh_values)


def ring_order(count):
    inner = max(d for d in range(1, count + 1) if count % d == 0 and d * d <= count)
    outer = count // inner
    if inner == 1:
        return list(range(count))
    order = [z * inner for z in range(outer)]
    for turn, z in enumerate(reversed(range(outer))):
        columns = list(range(1, inner))
        if turn % 2:
            columns.reverse()
        order += [z * inner + c for c in columns]
    return order


def ring_step(blocks, step, order, chunk):
    count = len(order)
    up = [(order[i], order[(i + 1) % count]) for i in range(count)]
    down = [(b, a) for a, b in up]
    if step < count // 2 or chunk % 2 == 0:
        blocks[count - step] = lax.ppermute(blocks[(1 - step) % count], "fsdp", up)
    if step < count // 2 or chunk % 2 == 1:
        blocks[step] = lax.ppermute(blocks[step - 1], "fsdp", down)


def facts_table(count, own_width, width):
    order = ring_order(count)
    position = {f: i for i, f in enumerate(order)}
    half = count // 2
    rows = []
    for chip in range(count):
        for core in range(2):
            side, mine = chip // half, chip % half
            start = mine // 2 * 2 * own_width
            owner = start // width if core == side else -1
            places = [order[(position[chip] + i) % count] for i in range(count)]
            rows.append([core, core ^ side, mine, owner, start % width, chip % 2] + places)
    return np.array(rows, np.int32)


fact_core, fact_kept, fact_mine, fact_owner, fact_start, fact_odd, fact_places = range(7)


def collect(facts, blocks, held, columns):
    for offset, ref in enumerate(blocks):
        held[facts[fact_places + offset]] = ref[:, columns]


def rank_kernel(count, facts, *refs):
    chunks, refs = refs[: chunk_count * count], refs[chunk_count * count :]
    factors, (ranked, held, factor) = refs[:4], refs[4:]
    width = held.shape[2]
    half, each = factors[0].shape
    ranked[...] = jnp.zeros_like(ranked)
    for chunk in range(chunk_count):
        blocks = chunks[chunk * count : (chunk + 1) * count]

        @pl.when(facts[fact_owner] == chunk)
        def _():
            start = pl.multiple_of(facts[fact_start], 128)
            collect(facts, blocks, held, pl.ds(start, width))
            core, odd = facts[fact_core], facts[fact_odd]
            for index, ref in enumerate(factors):
                row = core ^ (index // 2)
                column = odd ^ (index % 2)
                factor[
                    pl.ds(pl.multiple_of(row * half, half), half),
                    pl.ds(pl.multiple_of(column * each, each), each),
                ] = ref[...]
            ranked[...] = lax.dot_general(
                held[...].reshape(-1, width),
                factor[...],
                (((1,), (1,)), ((), ())),
                preferred_element_type=jnp.float32,
            )


def rank_part(facts, gathered, factors):
    blocks = [x for chunk in gathered for x in chunk]
    count = len(gathered[0])
    block_rows = blocks[0].shape[0]
    half, each = factors[0].shape
    vmem = pl.BlockSpec(memory_space=pltpu.VMEM)
    return pl.pallas_call(
        functools.partial(rank_kernel, count),
        in_specs=[pl.BlockSpec(memory_space=pltpu.SMEM)] + [vmem] * (len(blocks) + 4),
        out_specs=vmem,
        out_shape=jax.ShapeDtypeStruct((count * block_rows, 2 * half), jnp.float32),
        scratch_shapes=[
            pltpu.VMEM((count, block_rows, 2 * each), jnp.bfloat16),
            pltpu.VMEM((2 * half, 2 * each), jnp.bfloat16),
        ],
        compiler_params=pltpu.CompilerParams(vmem_limit_bytes=8 * mebibyte),
        cost_estimate=pl.CostEstimate(
            flops=8 * count * block_rows * half * each, bytes_accessed=mebibyte, transcendentals=0
        ),
        name="rank_part",
    )(facts, *blocks, *factors)


def project_kernel(count, facts, *refs):
    chunks, refs = refs[: chunk_count * count], refs[chunk_count * count :]
    weight, keep, send, held, streamed, sems = refs
    width = held.shape[2]
    rows = held.shape[0] * held.shape[1]
    edges = [weight.shape[0] * i // 16 for i in weight_edges]
    copies = [
        pltpu.make_async_copy(
            weight.at[pl.ds(first, last - first), :],
            streamed.at[pl.ds(first, last - first), :],
            sems.at[i],
        )
        for i, (first, last) in enumerate(zip(edges, edges[1:]))
    ]
    for copy in copies:
        copy.start()
    total = None
    chunk = None
    for copy, first, last in zip(copies, edges, edges[1:]):
        if first // width != chunk:
            chunk = first // width
            collect(facts, chunks[chunk * count : (chunk + 1) * count], held, slice(None))
        copy.wait()
        start = first - chunk * width
        part = jnp.dot(
            held[:, :, start : start + last - first].reshape(rows, last - first),
            streamed[first:last, :],
            preferred_element_type=jnp.float32,
        )
        total = part if total is None else total + part
    kept = facts[fact_kept]
    top, bottom = total[: rows // 2], total[rows // 2 :]
    keep[...] = jnp.where(kept == 0, top, bottom)
    send[...] = jnp.where(kept == 0, bottom, top)


def project(facts, gathered, base_weight):
    blocks = [x for chunk in gathered for x in chunk]
    count = len(gathered[0])
    block_rows, width = blocks[0].shape
    columns = base_weight.shape[1]
    rows = count * block_rows
    vmem = pl.BlockSpec(memory_space=pltpu.VMEM)
    return pl.pallas_call(
        functools.partial(project_kernel, count),
        in_specs=[pl.BlockSpec(memory_space=pltpu.SMEM)] + [vmem] * len(blocks) + [pl.BlockSpec(memory_space=pl.ANY)],
        out_specs=[vmem] * 2,
        out_shape=[jax.ShapeDtypeStruct((rows // 2, columns), jnp.float32)] * 2,
        scratch_shapes=[
            pltpu.VMEM((count, block_rows, width), jnp.bfloat16),
            pltpu.VMEM(base_weight.shape, jnp.bfloat16),
            pltpu.SemaphoreType.DMA((len(weight_edges) - 1,)),
        ],
        compiler_params=pltpu.CompilerParams(vmem_limit_bytes=48 * mebibyte),
        cost_estimate=pl.CostEstimate(
            flops=2 * rows * chunk_count * width * columns,
            bytes_accessed=2 * chunk_count * width * columns,
            transcendentals=0,
        ),
        name="project",
    )(facts, *blocks, base_weight)


def add_kernel(a, b, out):
    out[...] = a[...] + b[...]


def add(a, b):
    vmem = pl.BlockSpec(memory_space=pltpu.VMEM)
    return pl.pallas_call(
        add_kernel,
        in_specs=[vmem] * 2,
        out_specs=vmem,
        out_shape=jax.ShapeDtypeStruct(a.shape, a.dtype),
        compiler_params=pltpu.CompilerParams(vmem_limit_bytes=4 * mebibyte),
        name="add",
    )(a, b)


def split_kernel(facts, a, b, keep, send):
    rows = keep.shape[0]
    total = a[...] + b[...]
    kept = facts[fact_kept]
    keep[...] = jnp.where(kept == 0, total[:rows], total[rows:])
    send[...] = jnp.where(kept == 0, total[rows:], total[:rows])


def split(facts, a, b):
    vmem = pl.BlockSpec(memory_space=pltpu.VMEM)
    return pl.pallas_call(
        split_kernel,
        in_specs=[pl.BlockSpec(memory_space=pltpu.SMEM)] + [vmem] * 2,
        out_specs=[vmem] * 2,
        out_shape=[jax.ShapeDtypeStruct((a.shape[0] // 2, a.shape[1]), a.dtype)] * 2,
        compiler_params=pltpu.CompilerParams(vmem_limit_bytes=4 * mebibyte),
        name="split",
    )(facts, a, b)


def finish_kernel(facts, keep, received, ranked, ranked_received, own, other, *refs):
    *outs, factor = refs
    half = own.shape[0]
    core = facts[fact_core]
    for part in range(2):
        base = 2 * half * part
        factor[pl.ds(pl.multiple_of(base + core * half, half), half), :] = own[...]
        factor[pl.ds(pl.multiple_of(base + (1 - core) * half, half), half), :] = other[...]
    scaled = adapter_scale * (ranked[...] + ranked_received[...])
    high = scaled.astype(jnp.bfloat16)
    low = (scaled - high.astype(jnp.float32)).astype(jnp.bfloat16)
    pair = jnp.concatenate([high, low], axis=1)
    added = jnp.dot(pair, factor[...], preferred_element_type=jnp.float32)
    total = (keep[...] + received[...] + added).astype(jnp.bfloat16)
    block = keep.shape[0] // len(outs)
    mine = facts[fact_mine]
    for index in range(len(outs)):
        for offset, out in enumerate(outs):

            @pl.when(mine ^ offset == index)
            def _():
                out[...] = total[index * block : (index + 1) * block].reshape(out.shape)


def finish(facts, keep, received, ranked, ranked_received, own, other, row_count, step_count):
    rows, columns = keep.shape
    pieces = rows // (row_count * step_count)
    vmem = pl.BlockSpec(memory_space=pltpu.VMEM)
    return pl.pallas_call(
        finish_kernel,
        in_specs=[pl.BlockSpec(memory_space=pltpu.SMEM)] + [vmem] * 6,
        out_specs=[vmem] * pieces,
        out_shape=[jax.ShapeDtypeStruct((row_count, step_count, columns), jnp.bfloat16)] * pieces,
        scratch_shapes=[pltpu.VMEM((4 * own.shape[0], columns), jnp.bfloat16)],
        compiler_params=pltpu.CompilerParams(vmem_limit_bytes=16 * mebibyte),
        name="finish",
    )(facts, keep, received, ranked, ranked_received, own, other)


def place_kernel(facts, *refs):
    *pieces, out, sems = refs
    mine = facts[fact_mine]
    copies = []
    for offset, ref in enumerate(pieces):
        width = ref.shape[2]
        columns = pl.ds(pl.multiple_of((mine ^ offset) * width, width), width)
        copies.append(pltpu.make_async_copy(ref, out.at[:, :, columns], sems.at[offset]))
    for copy in copies:
        copy.start()
    for copy in copies:
        copy.wait()


def place(facts, pieces):
    row_count, step_count, width = pieces[0].shape
    anywhere = pl.BlockSpec(memory_space=pl.ANY)
    return pl.pallas_call(
        place_kernel,
        in_specs=[pl.BlockSpec(memory_space=pltpu.SMEM)] + [anywhere] * len(pieces),
        out_specs=anywhere,
        out_shape=jax.ShapeDtypeStruct((row_count, step_count, width * len(pieces)), jnp.bfloat16),
        scratch_shapes=[pltpu.SemaphoreType.DMA((len(pieces),))],
        compiler_params=pltpu.CompilerParams(vmem_limit_bytes=4 * mebibyte),
        name="place",
    )(facts, *pieces)


def shards(
    count,
    queries,
    cache_keys,
    cache_values,
    new_keys,
    new_values,
    cache_lengths,
    base_weight,
    factor_in,
    adapter_output_factor,
):
    order = ring_order(count)
    half = count // 2
    both = ("fsdp", "tp")
    swap = [(0, 1), (1, 0)]
    after = lax.optimization_barrier
    row_count, step_count, head_count, head_width = queries.shape
    slots, key_heads = cache_keys.shape[1:3]
    own_width = factor_in.shape[0]
    width = head_count * head_width // chunk_count
    facts = lax.dynamic_index_in_dim(
        jnp.asarray(facts_table(count, own_width, width)),
        lax.axis_index(both).astype(jnp.int32),
        0,
        keepdims=False,
    )

    own_in, own_out = factor_in.T, adapter_output_factor
    near_in = lax.ppermute(own_in, "fsdp", [(f, f ^ 1) for f in range(count)])
    attended = attend(
        cache_lengths,
        queries,
        cache_keys.reshape(row_count, slots * key_heads, head_width),
        cache_values.reshape(row_count, slots * key_heads, head_width),
        new_keys.reshape(row_count, step_count * key_heads, head_width),
        new_values.reshape(row_count, step_count * key_heads, head_width),
    )
    attended, near_in, facts = after((attended, near_in, facts))
    gathered = [[x] * count for x in attended]
    for step in range(1, half + 1):
        for c, blocks in enumerate(gathered):
            ring_step(blocks, step, order, c)
        if step == 2:
            others = [lax.ppermute(x, "tp", swap) for x in (own_in, near_in, own_out)]
            gathered[0][count - 2], others = after((gathered[0][count - 2], others))
    other_in, other_near_in, other_out = others

    ranked = rank_part(facts, gathered, (own_in, near_in, other_in, other_near_in))
    bit, keep = 2, None
    while True:
        if bit < half:
            pairs = [(2 * f + f // half, 2 * (f ^ bit) + f // half) for f in range(count)]
        else:
            pairs = [(2 * f + f // half, 2 * (f ^ half) + f // half) for f in range(count)]
        received = lax.ppermute(ranked, both, pairs)
        if keep is None:
            keep, send = project(facts, gathered, base_weight)
            received, keep, send = after((received, keep, send))
        if bit >= half:
            break
        ranked = add(ranked, received)
        bit *= 2
    ranked_keep, ranked_send = split(facts, ranked, received)
    ranked_received = lax.ppermute(ranked_send, "tp", swap)
    received = lax.ppermute(send, "tp", swap)
    pieces = finish(
        facts, keep, received, ranked_keep, ranked_received, own_out, other_out, row_count, step_count
    )
    landed = []
    for offset, piece in enumerate(pieces):
        pairs = [
            (2 * f + t, 2 * (f ^ (t * half + offset)) + f // half)
            for f in range(count)
            for t in range(2)
        ]
        landed.append(lax.ppermute(piece, both, pairs))
    return place(facts, landed)


def solution(mesh):
    return jax.shard_map(
        functools.partial(shards, mesh.shape["fsdp"]),
        mesh=mesh,
        in_specs=(
            P(("groups", "fsdp"), None, "tp", None),
            P(("groups", "fsdp"), None, "tp", None),
            P(("groups", "fsdp"), None, "tp", None),
            P(("groups", "fsdp"), None, "tp", None),
            P(("groups", "fsdp"), None, "tp", None),
            P(("groups", "fsdp")),
            P("tp", "fsdp"),
            P(("groups", "fsdp"), "tp"),
            P(("groups", "tp"), "fsdp"),
        ),
        out_specs=P(("groups", "fsdp"), None, "tp"),
        check_vma=False,
    )
```

```python
import functools
import math

import jax
import jax.numpy as jnp
import numpy as np
from jax import lax
from jax.experimental import pallas as pl
from jax.experimental.pallas import tpu as pltpu
from jax.sharding import PartitionSpec as P

adapter_scale = 2.0
chunk_count = 2
fetched = 64
staged_rows = 2
weight_edges = (0, 3, 8, 13, 16)
mebibyte = 1024 * 1024


def attend_kernel(
    lengths, queries, keys, values, fresh_keys, fresh_values, *refs
):
    outs, refs = refs[:chunk_count], refs[chunk_count:]
    query_held, key_held, value_held, fresh_key_held, fresh_value_held, key_wide, value_wide, gathered, sems = refs
    row_count, step_count, heads, head_width = query_held.shape
    old_rows, new_rows = key_held.shape[1], fresh_key_held.shape[1]
    groups = new_rows // step_count
    per_group = heads // groups
    slots = old_rows // groups
    columns = key_wide.shape[1] // groups
    rows = step_count * per_group
    exponent_scale = math.log2(math.e) / math.sqrt(head_width)

    fresh = [
        pltpu.make_async_copy(fresh_keys, fresh_key_held, sems.at[0]),
        pltpu.make_async_copy(queries, query_held, sems.at[1]),
        pltpu.make_async_copy(fresh_values, fresh_value_held, sems.at[2]),
    ]
    old_keys = [
        pltpu.make_async_copy(keys.at[row], key_held.at[row], sems.at[3 + row])
        for row in range(row_count)
    ]
    old_values = [
        pltpu.make_async_copy(values.at[row], value_held.at[row], sems.at[3 + row_count + row])
        for row in range(row_count)
    ]
    for copy in fresh:
        copy.start()
    for row in range(min(staged_rows, row_count)):
        old_keys[row].start()
        old_values[row].start()
    for copy in fresh:
        copy.wait()

    column = lax.broadcasted_iota(jnp.int32, (step_count, 1, columns), 2)
    step = lax.broadcasted_iota(jnp.int32, (step_count, 1, columns), 0)
    fresh_seen = (column >= slots) & (column - slots <= step)

    def widen(old, new, wide):
        wide[:old_rows] = old.astype(jnp.float32)
        wide[old_rows : old_rows + new_rows] = new.astype(jnp.float32)
        wide[old_rows + new_rows :] = jnp.zeros_like(wide[old_rows + new_rows :])

    def picked(group):
        return pl.ds(group, columns, stride=groups)

    for row in range(row_count):
        old_keys[row].wait()
        widen(key_held[row], fresh_key_held[row], key_wide.at[row])
        bias = jnp.where((column < jnp.minimum(lengths[row], slots)) | fresh_seen, 0.0, -jnp.inf)
        scores = [
            lax.dot_general(
                query_held[row, :, group * per_group : (group + 1) * per_group, :].reshape(
                    rows, head_width
                ),
                key_wide[row, picked(group), :].astype(jnp.bfloat16),
                (((1,), (1,)), ((), ())),
                preferred_element_type=jnp.float32,
            ).reshape(step_count, per_group, columns)
            + bias
            for group in range(groups)
        ]
        old_values[row].wait()
        if row + staged_rows < row_count:
            old_keys[row + staged_rows].start()
            old_values[row + staged_rows].start()
        widen(value_held[row], fresh_value_held[row], value_wide.at[row])
        tops = [score.max(-1, keepdims=True) for score in scores]
        scores = [
            jnp.exp2((score - top) * exponent_scale) for score, top in zip(scores, tops)
        ]
        totals = [score.sum(-1, keepdims=True) for score in scores]
        weighted = [
            jnp.dot(
                score.astype(jnp.bfloat16).reshape(rows, columns),
                value_wide[row, picked(group), :].astype(jnp.bfloat16),
                preferred_element_type=jnp.float32,
            ).reshape(step_count, per_group, head_width)
            for group, score in enumerate(scores)
        ]
        for group in range(groups):
            result = weighted[group] / totals[group]
            for s in range(step_count):
                place = (row * step_count + s) * heads + group * per_group
                gathered[place : place + per_group, :] = result[s]
    each = heads // chunk_count
    for head in range(heads):
        place = head % each * head_width
        outs[head // each][:, place : place + head_width] = gathered[
            pl.ds(head, row_count * step_count, stride=heads), :
        ].astype(jnp.bfloat16)


def attend(lengths, queries, keys, values, fresh_keys, fresh_values):
    row_count, step_count, heads, head_width = queries.shape
    smem = pl.BlockSpec(memory_space=pltpu.SMEM)
    vmem = pl.BlockSpec(memory_space=pltpu.VMEM)
    anywhere = pl.BlockSpec(memory_space=pl.ANY)
    kind = jnp.bfloat16
    shape = (row_count * step_count, heads * head_width // chunk_count)
    groups = fresh_keys.shape[1] // step_count
    columns = -(-(keys.shape[1] + fresh_keys.shape[1]) // (16 * groups)) * 16
    wide = pltpu.VMEM((row_count, columns * groups, head_width), jnp.float32)
    return pl.pallas_call(
        attend_kernel,
        in_specs=[smem] + [anywhere] * 5,
        out_specs=[vmem] * chunk_count,
        out_shape=[jax.ShapeDtypeStruct(shape, kind)] * chunk_count,
        scratch_shapes=[
            pltpu.VMEM(queries.shape, kind),
            pltpu.VMEM(keys.shape, kind),
            pltpu.VMEM(values.shape, kind),
            pltpu.VMEM(fresh_keys.shape, kind),
            pltpu.VMEM(fresh_values.shape, kind),
            wide,
            wide,
            pltpu.VMEM((row_count * step_count * heads, head_width), jnp.float32),
            pltpu.SemaphoreType.DMA((3 + 2 * row_count,)),
        ],
        compiler_params=pltpu.CompilerParams(vmem_limit_bytes=58 * mebibyte),
        cost_estimate=pl.CostEstimate(
            flops=4 * row_count * step_count * heads * keys.shape[1] * head_width,
            bytes_accessed=4 * keys.size,
            transcendentals=row_count * step_count * heads * keys.shape[1],
        ),
        name="attend",
    )(lengths, queries, keys, values, fresh_keys, fresh_values)


def ring_order(count):
    inner = max(d for d in range(1, count + 1) if count % d == 0 and d * d <= count)
    outer = count // inner
    if inner == 1:
        return list(range(count))
    order = [z * inner for z in range(outer)]
    for turn, z in enumerate(reversed(range(outer))):
        columns = list(range(1, inner))
        if turn % 2:
            columns.reverse()
        order += [z * inner + c for c in columns]
    return order


def ring_step(blocks, step, order, chunk):
    count = len(order)
    up = [(order[i], order[(i + 1) % count]) for i in range(count)]
    down = [(b, a) for a, b in up]
    if step < count // 2 or chunk % 2 == 0:
        blocks[count - step] = lax.ppermute(blocks[(1 - step) % count], "fsdp", up)
    if step < count // 2 or chunk % 2 == 1:
        blocks[step] = lax.ppermute(blocks[step - 1], "fsdp", down)


def facts_table(count, own_width, width):
    order = ring_order(count)
    position = {f: i for i, f in enumerate(order)}
    half = count // 2
    rows = []
    for chip in range(count):
        for core in range(2):
            side, mine = chip // half, chip % half
            start = mine // 2 * 2 * own_width
            owner = start // width if core == side else -1
            places = [order[(position[chip] + i) % count] for i in range(count)]
            rows.append([core, core ^ side, mine, owner, start % width, chip % 2] + places)
    return np.array(rows, np.int32)


fact_core, fact_kept, fact_mine, fact_owner, fact_start, fact_odd, fact_places = range(7)


def collect(facts, blocks, held, columns, sem):
    own = pltpu.make_async_copy(blocks[0].at[:, columns], held.at[facts[fact_places]], sem)
    own.start()
    for offset, ref in enumerate(blocks[1:]):
        held[facts[fact_places + 1 + offset]] = ref[:, columns]
    own.wait()


def block_specs(count):
    vmem = pl.BlockSpec(memory_space=pltpu.VMEM)
    return [pl.BlockSpec(memory_space=pl.ANY)] + [vmem] * (count - 1)


def fetch_kernel(weight, *refs):
    out, token, sem = refs[-3:]
    copy = pltpu.make_async_copy(weight.at[pl.ds(0, out.shape[0]), :], out, sem)
    copy.start()
    token[...] = jnp.zeros_like(token)
    copy.wait()


def fetch(base_weight, after):
    rows, columns = base_weight.shape
    vmem = pl.BlockSpec(memory_space=pltpu.VMEM)
    rows = rows * fetched // 256
    return pl.pallas_call(
        fetch_kernel,
        in_specs=[pl.BlockSpec(memory_space=pl.ANY)] * (1 + len(after)),
        out_specs=[vmem] * 2,
        out_shape=[
            jax.ShapeDtypeStruct((rows, columns), base_weight.dtype),
            jax.ShapeDtypeStruct((8, 128), jnp.float32),
        ],
        scratch_shapes=[pltpu.SemaphoreType.DMA(())],
        compiler_params=pltpu.CompilerParams(vmem_limit_bytes=24 * mebibyte),
        cost_estimate=pl.CostEstimate(flops=0, bytes_accessed=4 * rows * columns, transcendentals=0),
        name="fetch",
    )(base_weight, *after)


def rank_kernel(count, facts, _, *refs):
    chunks, refs = refs[: chunk_count * count], refs[chunk_count * count :]
    factors, (ranked, held, factor, sem) = refs[:4], refs[4:]
    width = held.shape[2]
    half, each = factors[0].shape
    ranked[...] = jnp.zeros_like(ranked)
    for chunk in range(chunk_count):
        blocks = chunks[chunk * count : (chunk + 1) * count]

        @pl.when(facts[fact_owner] == chunk)
        def _():
            start = pl.multiple_of(facts[fact_start], 128)
            collect(facts, blocks, held, pl.ds(start, width), sem)
            core, odd = facts[fact_core], facts[fact_odd]
            for index, ref in enumerate(factors):
                row = core ^ (index // 2)
                column = odd ^ (index % 2)
                factor[
                    pl.ds(pl.multiple_of(row * half, half), half),
                    pl.ds(pl.multiple_of(column * each, each), each),
                ] = ref[...]
            ranked[...] = lax.dot_general(
                held[...].reshape(-1, width),
                factor[...],
                (((1,), (1,)), ((), ())),
                preferred_element_type=jnp.float32,
            )


def rank_part(facts, token, gathered, factors):
    blocks = [x for chunk in gathered for x in chunk]
    count = len(gathered[0])
    block_rows = blocks[0].shape[0]
    half, each = factors[0].shape
    vmem = pl.BlockSpec(memory_space=pltpu.VMEM)
    return pl.pallas_call(
        functools.partial(rank_kernel, count),
        in_specs=[pl.BlockSpec(memory_space=pltpu.SMEM), pl.BlockSpec(memory_space=pl.ANY)]
        + block_specs(count) * chunk_count
        + [vmem] * 4,
        out_specs=vmem,
        out_shape=jax.ShapeDtypeStruct((count * block_rows, 2 * half), jnp.float32),
        scratch_shapes=[
            pltpu.VMEM((count, block_rows, 2 * each), jnp.bfloat16),
            pltpu.VMEM((2 * half, 2 * each), jnp.bfloat16),
            pltpu.SemaphoreType.DMA(()),
        ],
        compiler_params=pltpu.CompilerParams(vmem_limit_bytes=47 * mebibyte),
        cost_estimate=pl.CostEstimate(
            flops=8 * count * block_rows * half * each, bytes_accessed=mebibyte, transcendentals=0
        ),
        name="rank_part",
    )(facts, token, *blocks, *factors)


def project_kernel(chunk, facts, *refs):
    refs = list(refs)
    held, streamed, sem, sems = refs[-4:]
    last = chunk == chunk_count - 1
    outs = refs[-5 - last : -4]
    refs = refs[: -5 - last]
    previous = refs.pop() if chunk else None
    weight = refs.pop()
    ready = None if chunk else refs.pop()
    width = held.shape[2]
    rows = held.shape[0] * held.shape[1]
    skipped = 0 if chunk else ready.shape[0]
    edges = [skipped + (width - skipped) * i // 16 for i in weight_edges]
    copies = [
        pltpu.make_async_copy(
            weight.at[pl.ds(chunk * width + start, stop - start), :],
            streamed.at[pl.ds(start - skipped, stop - start), :],
            sems.at[i],
        )
        for i, (start, stop) in enumerate(zip(edges, edges[1:]))
    ]
    for copy in copies:
        copy.start()
    collect(facts, refs, held, slice(None), sem)

    def product(start, stop, factor):
        return jnp.dot(
            held[:, :, start:stop].reshape(rows, stop - start),
            factor,
            preferred_element_type=jnp.float32,
        )

    total = previous[...] if chunk else product(0, skipped, ready[...])
    for copy, start, stop in zip(copies, edges, edges[1:]):
        copy.wait()
        total += product(start, stop, streamed[start - skipped : stop - skipped, :])
    if not last:
        outs[0][...] = total
        return
    keep, send = outs
    kept = facts[fact_kept]
    top, bottom = total[: rows // 2], total[rows // 2 :]
    keep[...] = jnp.where(kept == 0, top, bottom)
    send[...] = jnp.where(kept == 0, bottom, top)


def project(chunk, facts, blocks, ready, base_weight, previous):
    count = len(blocks)
    block_rows, width = blocks[0].shape
    columns = base_weight.shape[1]
    rows = count * block_rows
    last = chunk == chunk_count - 1
    vmem = pl.BlockSpec(memory_space=pltpu.VMEM)
    anywhere = pl.BlockSpec(memory_space=pl.ANY)
    result = pl.pallas_call(
        functools.partial(project_kernel, chunk),
        in_specs=[pl.BlockSpec(memory_space=pltpu.SMEM)]
        + block_specs(count)
        + [vmem] * (chunk == 0)
        + [anywhere]
        + [vmem] * (chunk > 0),
        out_specs=[vmem] * (1 + last),
        out_shape=[jax.ShapeDtypeStruct((rows // (1 + last), columns), jnp.float32)] * (1 + last),
        scratch_shapes=[
            pltpu.VMEM((count, block_rows, width), jnp.bfloat16),
            pltpu.VMEM((width if chunk else width - ready.shape[0], columns), jnp.bfloat16),
            pltpu.SemaphoreType.DMA(()),
            pltpu.SemaphoreType.DMA((len(weight_edges) - 1,)),
        ],
        compiler_params=pltpu.CompilerParams(vmem_limit_bytes=(32 if chunk else 26) * mebibyte),
        cost_estimate=pl.CostEstimate(
            flops=2 * rows * width * columns, bytes_accessed=2 * width * columns, transcendentals=0
        ),
        name=f"project_{chunk}",
    )(facts, *blocks, *([] if chunk else [ready]), base_weight, *([previous] if chunk else []))
    return result if last else result[0]


def add_kernel(a, b, out):
    out[...] = a[...] + b[...]


def add(a, b):
    vmem = pl.BlockSpec(memory_space=pltpu.VMEM)
    return pl.pallas_call(
        add_kernel,
        in_specs=[vmem] * 2,
        out_specs=vmem,
        out_shape=jax.ShapeDtypeStruct(a.shape, a.dtype),
        compiler_params=pltpu.CompilerParams(vmem_limit_bytes=4 * mebibyte),
        name="add",
    )(a, b)


def split_kernel(facts, a, b, keep, send):
    rows = keep.shape[0]
    total = a[...] + b[...]
    kept = facts[fact_kept]
    keep[...] = jnp.where(kept == 0, total[:rows], total[rows:])
    send[...] = jnp.where(kept == 0, total[rows:], total[:rows])


def split(facts, a, b):
    vmem = pl.BlockSpec(memory_space=pltpu.VMEM)
    return pl.pallas_call(
        split_kernel,
        in_specs=[pl.BlockSpec(memory_space=pltpu.SMEM)] + [vmem] * 2,
        out_specs=[vmem] * 2,
        out_shape=[jax.ShapeDtypeStruct((a.shape[0] // 2, a.shape[1]), a.dtype)] * 2,
        compiler_params=pltpu.CompilerParams(vmem_limit_bytes=4 * mebibyte),
        name="split",
    )(facts, a, b)


def finish_kernel(facts, keep, received, ranked, ranked_received, own, other, *refs):
    *outs, factor = refs
    half = own.shape[0]
    core = facts[fact_core]
    for part in range(2):
        base = 2 * half * part
        factor[pl.ds(pl.multiple_of(base + core * half, half), half), :] = own[...]
        factor[pl.ds(pl.multiple_of(base + (1 - core) * half, half), half), :] = other[...]
    scaled = adapter_scale * (ranked[...] + ranked_received[...])
    high = scaled.astype(jnp.bfloat16)
    low = (scaled - high.astype(jnp.float32)).astype(jnp.bfloat16)
    pair = jnp.concatenate([high, low], axis=1)
    added = jnp.dot(pair, factor[...], preferred_element_type=jnp.float32)
    total = (keep[...] + received[...] + added).astype(jnp.bfloat16)
    block = keep.shape[0] // len(outs)
    mine = facts[fact_mine]
    for index in range(len(outs)):
        for offset, out in enumerate(outs):

            @pl.when(mine ^ offset == index)
            def _():
                out[...] = total[index * block : (index + 1) * block].reshape(out.shape)


def finish(facts, keep, received, ranked, ranked_received, own, other, row_count, step_count):
    rows, columns = keep.shape
    pieces = rows // (row_count * step_count)
    vmem = pl.BlockSpec(memory_space=pltpu.VMEM)
    return pl.pallas_call(
        finish_kernel,
        in_specs=[pl.BlockSpec(memory_space=pltpu.SMEM)] + [vmem] * 6,
        out_specs=[vmem] * pieces,
        out_shape=[jax.ShapeDtypeStruct((row_count, step_count, columns), jnp.bfloat16)] * pieces,
        scratch_shapes=[pltpu.VMEM((4 * own.shape[0], columns), jnp.bfloat16)],
        compiler_params=pltpu.CompilerParams(vmem_limit_bytes=16 * mebibyte),
        name="finish",
    )(facts, keep, received, ranked, ranked_received, own, other)


def place_kernel(facts, *refs):
    *pieces, out, sems = refs
    mine = facts[fact_mine]
    copies = []
    for offset, ref in enumerate(pieces):
        width = ref.shape[2]
        columns = pl.ds(pl.multiple_of((mine ^ offset) * width, width), width)
        copies.append(pltpu.make_async_copy(ref, out.at[:, :, columns], sems.at[offset]))
    for copy in copies:
        copy.start()
    for copy in copies:
        copy.wait()


def place(facts, pieces):
    row_count, step_count, width = pieces[0].shape
    anywhere = pl.BlockSpec(memory_space=pl.ANY)
    return pl.pallas_call(
        place_kernel,
        in_specs=[pl.BlockSpec(memory_space=pltpu.SMEM)] + [anywhere] * len(pieces),
        out_specs=anywhere,
        out_shape=jax.ShapeDtypeStruct((row_count, step_count, width * len(pieces)), jnp.bfloat16),
        scratch_shapes=[pltpu.SemaphoreType.DMA((len(pieces),))],
        compiler_params=pltpu.CompilerParams(vmem_limit_bytes=4 * mebibyte),
        name="place",
    )(facts, *pieces)


def shards(
    count,
    queries,
    cache_keys,
    cache_values,
    new_keys,
    new_values,
    cache_lengths,
    base_weight,
    factor_in,
    adapter_output_factor,
):
    order = ring_order(count)
    half = count // 2
    both = ("fsdp", "tp")
    swap = [(0, 1), (1, 0)]
    after = lax.optimization_barrier
    row_count, step_count, head_count, head_width = queries.shape
    slots, key_heads = cache_keys.shape[1:3]
    own_width = factor_in.shape[0]
    width = head_count * head_width // chunk_count
    facts = lax.dynamic_index_in_dim(
        jnp.asarray(facts_table(count, own_width, width)),
        lax.axis_index(both).astype(jnp.int32),
        0,
        keepdims=False,
    )

    own_in, own_out = factor_in.T, adapter_output_factor
    near_in = lax.ppermute(own_in, "fsdp", [(f, f ^ 1) for f in range(count)])
    attended = attend(
        cache_lengths,
        queries,
        cache_keys.reshape(row_count, slots * key_heads, head_width),
        cache_values.reshape(row_count, slots * key_heads, head_width),
        new_keys.reshape(row_count, step_count * key_heads, head_width),
        new_values.reshape(row_count, step_count * key_heads, head_width),
    )
    attended, near_in = after((attended, near_in))
    gathered = [[x] * count for x in attended]
    for step in range(1, half + 1):
        for c, blocks in enumerate(gathered):
            ring_step(blocks, step, order, c)
        if step == 2:
            others = [lax.ppermute(x, "tp", swap) for x in (own_in, near_in, own_out)]
            gathered[0][count - 2], others = after((gathered[0][count - 2], others))
    other_in, other_near_in, other_out = others
    sent = [blocks[i] for blocks in gathered for i in (half - 1, half + 1)]
    ready, token = fetch(base_weight, sent)
    gathered[-1][half], token = after((gathered[-1][half], token))

    ranked = rank_part(facts, token, gathered, (own_in, near_in, other_in, other_near_in))
    bit, done, state = 2, 0, None
    while True:
        last = bit >= half
        turn = half if last else bit
        pairs = [(2 * f + f // half, 2 * (f ^ turn) + f // half) for f in range(count)]
        received = lax.ppermute(ranked, both, pairs)
        while done < (chunk_count if last else 1):
            state = project(done, facts, gathered[done], ready, base_weight, state)
            done += 1
        received, state = after((received, state))
        if last:
            break
        ranked = add(ranked, received)
        bit *= 2
    keep, send = state
    ranked_keep, ranked_send = split(facts, ranked, received)
    ranked_received = lax.ppermute(ranked_send, "tp", swap)
    received = lax.ppermute(send, "tp", swap)
    pieces = finish(
        facts, keep, received, ranked_keep, ranked_received, own_out, other_out, row_count, step_count
    )
    landed = []
    for offset, piece in enumerate(pieces):
        pairs = [
            (2 * f + t, 2 * (f ^ (t * half + offset)) + f // half)
            for f in range(count)
            for t in range(2)
        ]
        landed.append(lax.ppermute(piece, both, pairs))
    return place(facts, landed)


def solution(mesh):
    return jax.shard_map(
        functools.partial(shards, mesh.shape["fsdp"]),
        mesh=mesh,
        in_specs=(
            P(("groups", "fsdp"), None, "tp", None),
            P(("groups", "fsdp"), None, "tp", None),
            P(("groups", "fsdp"), None, "tp", None),
            P(("groups", "fsdp"), None, "tp", None),
            P(("groups", "fsdp"), None, "tp", None),
            P(("groups", "fsdp")),
            P("tp", "fsdp"),
            P(("groups", "fsdp"), "tp"),
            P(("groups", "tp"), "fsdp"),
        ),
        out_specs=P(("groups", "fsdp"), None, "tp"),
        check_vma=False,
    )
```

```python
import functools
import math

import jax
import jax.numpy as jnp
import numpy as np
from jax import lax
from jax.experimental import pallas as pl
from jax.experimental.pallas import tpu as pltpu
from jax.sharding import PartitionSpec as P

adapter_scale = 2.0
chunk_count = 2
fetched = 64
ahead_share = 5
staged_rows = 2
tile_rows = 512
mebibyte = 1024 * 1024


def attend_kernel(
    lengths, queries, keys, values, fresh_keys, fresh_values, *refs
):
    outs, refs = refs[:chunk_count], refs[chunk_count:]
    query_held, key_held, value_held, fresh_key_held, fresh_value_held, key_wide, value_wide, gathered, sems = refs
    row_count, step_count, heads, head_width = query_held.shape
    old_rows, new_rows = key_held.shape[1], fresh_key_held.shape[1]
    groups = new_rows // step_count
    per_group = heads // groups
    slots = old_rows // groups
    columns = key_wide.shape[1] // groups
    rows = step_count * per_group
    exponent_scale = math.log2(math.e) / math.sqrt(head_width)

    fresh = [
        pltpu.make_async_copy(fresh_keys, fresh_key_held, sems.at[0]),
        pltpu.make_async_copy(queries, query_held, sems.at[1]),
        pltpu.make_async_copy(fresh_values, fresh_value_held, sems.at[2]),
    ]
    old_keys = [
        pltpu.make_async_copy(keys.at[row], key_held.at[row], sems.at[3 + row])
        for row in range(row_count)
    ]
    old_values = [
        pltpu.make_async_copy(values.at[row], value_held.at[row], sems.at[3 + row_count + row])
        for row in range(row_count)
    ]
    for copy in fresh:
        copy.start()
    for row in range(min(staged_rows, row_count)):
        old_keys[row].start()
        old_values[row].start()
    for copy in fresh:
        copy.wait()

    column = lax.broadcasted_iota(jnp.int32, (step_count, 1, columns), 2)
    step = lax.broadcasted_iota(jnp.int32, (step_count, 1, columns), 0)
    fresh_seen = (column >= slots) & (column - slots <= step)

    def widen(old, new, wide):
        wide[:old_rows] = old.astype(jnp.float32)
        wide[old_rows : old_rows + new_rows] = new.astype(jnp.float32)
        wide[old_rows + new_rows :] = jnp.zeros_like(wide[old_rows + new_rows :])

    def picked(group):
        return pl.ds(group, columns, stride=groups)

    for row in range(row_count):
        old_keys[row].wait()
        widen(key_held[row], fresh_key_held[row], key_wide.at[row])
        bias = jnp.where((column < jnp.minimum(lengths[row], slots)) | fresh_seen, 0.0, -jnp.inf)
        scores = [
            lax.dot_general(
                query_held[row, :, group * per_group : (group + 1) * per_group, :].reshape(
                    rows, head_width
                ),
                key_wide[row, picked(group), :].astype(jnp.bfloat16),
                (((1,), (1,)), ((), ())),
                preferred_element_type=jnp.float32,
            ).reshape(step_count, per_group, columns)
            + bias
            for group in range(groups)
        ]
        old_values[row].wait()
        if row + staged_rows < row_count:
            old_keys[row + staged_rows].start()
            old_values[row + staged_rows].start()
        widen(value_held[row], fresh_value_held[row], value_wide.at[row])
        tops = [score.max(-1, keepdims=True) for score in scores]
        scores = [
            jnp.exp2((score - top) * exponent_scale) for score, top in zip(scores, tops)
        ]
        totals = [score.sum(-1, keepdims=True) for score in scores]
        weighted = [
            jnp.dot(
                score.astype(jnp.bfloat16).reshape(rows, columns),
                value_wide[row, picked(group), :].astype(jnp.bfloat16),
                preferred_element_type=jnp.float32,
            ).reshape(step_count, per_group, head_width)
            for group, score in enumerate(scores)
        ]
        for group in range(groups):
            result = weighted[group] / totals[group]
            for s in range(step_count):
                place = (row * step_count + s) * heads + group * per_group
                gathered[place : place + per_group, :] = result[s]
    each = heads // chunk_count
    for head in range(heads):
        place = head % each * head_width
        outs[head // each][:, place : place + head_width] = gathered[
            pl.ds(head, row_count * step_count, stride=heads), :
        ].astype(jnp.bfloat16)


def attend(lengths, queries, keys, values, fresh_keys, fresh_values):
    row_count, step_count, heads, head_width = queries.shape
    smem = pl.BlockSpec(memory_space=pltpu.SMEM)
    vmem = pl.BlockSpec(memory_space=pltpu.VMEM)
    anywhere = pl.BlockSpec(memory_space=pl.ANY)
    kind = jnp.bfloat16
    shape = (row_count * step_count, heads * head_width // chunk_count)
    groups = fresh_keys.shape[1] // step_count
    columns = -(-(keys.shape[1] + fresh_keys.shape[1]) // (16 * groups)) * 16
    wide = pltpu.VMEM((row_count, columns * groups, head_width), jnp.float32)
    return pl.pallas_call(
        attend_kernel,
        in_specs=[smem] + [anywhere] * 5,
        out_specs=[vmem] * chunk_count,
        out_shape=[jax.ShapeDtypeStruct(shape, kind)] * chunk_count,
        scratch_shapes=[
            pltpu.VMEM(queries.shape, kind),
            pltpu.VMEM(keys.shape, kind),
            pltpu.VMEM(values.shape, kind),
            pltpu.VMEM(fresh_keys.shape, kind),
            pltpu.VMEM(fresh_values.shape, kind),
            wide,
            wide,
            pltpu.VMEM((row_count * step_count * heads, head_width), jnp.float32),
            pltpu.SemaphoreType.DMA((3 + 2 * row_count,)),
        ],
        compiler_params=pltpu.CompilerParams(vmem_limit_bytes=58 * mebibyte),
        cost_estimate=pl.CostEstimate(
            flops=4 * row_count * step_count * heads * keys.shape[1] * head_width,
            bytes_accessed=4 * keys.size,
            transcendentals=row_count * step_count * heads * keys.shape[1],
        ),
        name="attend",
    )(lengths, queries, keys, values, fresh_keys, fresh_values)


def ring_order(count):
    inner = max(d for d in range(1, count + 1) if count % d == 0 and d * d <= count)
    outer = count // inner
    if inner == 1:
        return list(range(count))
    order = [z * inner for z in range(outer)]
    for turn, z in enumerate(reversed(range(outer))):
        columns = list(range(1, inner))
        if turn % 2:
            columns.reverse()
        order += [z * inner + c for c in columns]
    return order


def ring_step(blocks, step, order, chunk):
    count = len(order)
    up = [(order[i], order[(i + 1) % count]) for i in range(count)]
    down = [(b, a) for a, b in up]
    if step < count // 2 or chunk % 2 == 0:
        blocks[count - step] = lax.ppermute(blocks[(1 - step) % count], "fsdp", up)
    if step < count // 2 or chunk % 2 == 1:
        blocks[step] = lax.ppermute(blocks[step - 1], "fsdp", down)


def facts_table(count, own_width, width):
    order = ring_order(count)
    position = {f: i for i, f in enumerate(order)}
    half = count // 2
    rows = []
    for chip in range(count):
        for core in range(2):
            side, mine = chip // half, chip % half
            start = mine // 2 * 2 * own_width
            owner = start // width if core == side else -1
            places = [order[(position[chip] + i) % count] for i in range(count)]
            rows.append([core, core ^ side, mine, owner, start % width, chip % 2] + places)
    return np.array(rows, np.int32)


fact_core, fact_kept, fact_mine, fact_owner, fact_start, fact_odd, fact_places = range(7)


def collect(facts, blocks, held, columns, sem):
    own = pltpu.make_async_copy(blocks[0].at[:, columns], held.at[facts[fact_places]], sem)
    own.start()
    for offset, ref in enumerate(blocks[1:]):
        held[facts[fact_places + 1 + offset]] = ref[:, columns]
    own.wait()


def block_specs(count):
    vmem = pl.BlockSpec(memory_space=pltpu.VMEM)
    return [pl.BlockSpec(memory_space=pl.ANY)] + [vmem] * (count - 1)


def fetch_kernel(weight, *refs):
    out, token, sem = refs[-3:]
    copy = pltpu.make_async_copy(weight.at[pl.ds(0, out.shape[0]), :], out, sem)
    copy.start()
    token[...] = jnp.zeros_like(token)
    copy.wait()


def fetch(base_weight, after):
    rows, columns = base_weight.shape
    vmem = pl.BlockSpec(memory_space=pltpu.VMEM)
    rows = rows * fetched // 256
    return pl.pallas_call(
        fetch_kernel,
        in_specs=[pl.BlockSpec(memory_space=pl.ANY)] * (1 + len(after)),
        out_specs=[vmem] * 2,
        out_shape=[
            jax.ShapeDtypeStruct((rows, columns), base_weight.dtype),
            jax.ShapeDtypeStruct((8, 128), jnp.float32),
        ],
        scratch_shapes=[pltpu.SemaphoreType.DMA(())],
        compiler_params=pltpu.CompilerParams(vmem_limit_bytes=24 * mebibyte),
        cost_estimate=pl.CostEstimate(flops=0, bytes_accessed=4 * rows * columns, transcendentals=0),
        name="fetch",
    )(base_weight, *after)


def rank_kernel(count, facts, _, *refs):
    chunks, refs = refs[: chunk_count * count], refs[chunk_count * count :]
    factors, (ranked, held, factor, sem) = refs[:4], refs[4:]
    width = held.shape[2]
    half, each = factors[0].shape
    ranked[...] = jnp.zeros_like(ranked)
    for chunk in range(chunk_count):
        blocks = chunks[chunk * count : (chunk + 1) * count]

        @pl.when(facts[fact_owner] == chunk)
        def _():
            start = pl.multiple_of(facts[fact_start], 128)
            collect(facts, blocks, held, pl.ds(start, width), sem)
            core, odd = facts[fact_core], facts[fact_odd]
            for index, ref in enumerate(factors):
                row = core ^ (index // 2)
                column = odd ^ (index % 2)
                factor[
                    pl.ds(pl.multiple_of(row * half, half), half),
                    pl.ds(pl.multiple_of(column * each, each), each),
                ] = ref[...]
            ranked[...] = lax.dot_general(
                held[...].reshape(-1, width),
                factor[...],
                (((1,), (1,)), ((), ())),
                preferred_element_type=jnp.float32,
            )


def rank_part(facts, token, gathered, factors):
    blocks = [x for chunk in gathered for x in chunk]
    count = len(gathered[0])
    block_rows = blocks[0].shape[0]
    half, each = factors[0].shape
    vmem = pl.BlockSpec(memory_space=pltpu.VMEM)
    return pl.pallas_call(
        functools.partial(rank_kernel, count),
        in_specs=[pl.BlockSpec(memory_space=pltpu.SMEM), pl.BlockSpec(memory_space=pl.ANY)]
        + block_specs(count) * chunk_count
        + [vmem] * 4,
        out_specs=vmem,
        out_shape=jax.ShapeDtypeStruct((count * block_rows, 2 * half), jnp.float32),
        scratch_shapes=[
            pltpu.VMEM((count, block_rows, 2 * each), jnp.bfloat16),
            pltpu.VMEM((2 * half, 2 * each), jnp.bfloat16),
            pltpu.SemaphoreType.DMA(()),
        ],
        compiler_params=pltpu.CompilerParams(vmem_limit_bytes=47 * mebibyte),
        cost_estimate=pl.CostEstimate(
            flops=8 * count * block_rows * half * each, bytes_accessed=mebibyte, transcendentals=0
        ),
        name="rank_part",
    )(facts, token, *blocks, *factors)


def project_kernel(start, stop, first, ahead, last, facts, *refs):
    refs = list(refs)
    held, streamed, sem, sems, ahead_sem = refs[-5:]
    count = held.shape[0]
    blocks, refs = refs[:count], refs[count:-5]
    ready, weight, refs = refs[0], refs[1], refs[2:]
    previous = refs.pop(0) if first else None
    width = stop - start
    rows = count * held.shape[1]
    skipped = ready.shape[0]
    edges = [*range(skipped, width, tile_rows), width]
    copies = [
        pltpu.make_async_copy(
            weight.at[pl.ds(first + begin, end - begin), :],
            streamed.at[pl.ds(begin - skipped, end - begin), :],
            sems.at[i],
        )
        for i, (begin, end) in enumerate(zip(edges, edges[1:]))
    ]
    for copy in copies:
        copy.start()
    if ahead:
        later = pltpu.make_async_copy(weight.at[pl.ds(first + width, ahead), :], refs[1], ahead_sem)
        later.start()
    collect(facts, blocks, held, slice(start, stop), sem)

    def product(begin, end, factor):
        return jnp.dot(
            held[:, :, begin:end].reshape(rows, end - begin),
            factor,
            preferred_element_type=jnp.float32,
        )

    total = product(0, skipped, ready[...])
    if first:
        total += previous[...]
    for copy, begin, end in zip(copies, edges, edges[1:]):
        copy.wait()
        total += product(begin, end, streamed[begin - skipped : end - skipped, :])
    if not last:
        refs[0][...] = total
        later.wait()
        return
    keep, send = refs
    kept = facts[fact_kept]
    top, bottom = total[: rows // 2], total[rows // 2 :]
    keep[...] = jnp.where(kept == 0, top, bottom)
    send[...] = jnp.where(kept == 0, bottom, top)


def project(facts, gathered, start, stop, ahead, ready, base_weight, previous):
    features, columns = base_weight.shape
    chunk_width = features // chunk_count
    chunk, start = divmod(start, chunk_width)
    stop = stop - chunk * chunk_width
    first = chunk * chunk_width + start
    blocks = gathered[chunk]
    count = len(blocks)
    block_rows = blocks[0].shape[0]
    rows = count * block_rows
    last = not ahead
    vmem = pl.BlockSpec(memory_space=pltpu.VMEM)
    shape = jax.ShapeDtypeStruct((rows // (1 + last), columns), jnp.float32)
    shapes = [shape] * 2 if last else [shape, jax.ShapeDtypeStruct((ahead, columns), jnp.bfloat16)]
    return pl.pallas_call(
        functools.partial(project_kernel, start, stop, first, ahead, last),
        in_specs=[pl.BlockSpec(memory_space=pltpu.SMEM)]
        + block_specs(count)
        + [vmem, pl.BlockSpec(memory_space=pl.ANY)]
        + [vmem] * (first > 0),
        out_specs=[vmem] * 2,
        out_shape=shapes,
        scratch_shapes=[
            pltpu.VMEM((count, block_rows, stop - start), jnp.bfloat16),
            pltpu.VMEM((stop - start - ready.shape[0], columns), jnp.bfloat16),
            pltpu.SemaphoreType.DMA(()),
            pltpu.SemaphoreType.DMA((-(-(stop - start - ready.shape[0]) // tile_rows),)),
            pltpu.SemaphoreType.DMA(()),
        ],
        compiler_params=pltpu.CompilerParams(vmem_limit_bytes=26 * mebibyte),
        cost_estimate=pl.CostEstimate(
            flops=2 * rows * (stop - start) * columns,
            bytes_accessed=2 * (stop - start) * columns,
            transcendentals=0,
        ),
        name=f"project_{first}",
    )(facts, *blocks, ready, base_weight, *([previous] if first else []))


def add_kernel(a, b, out):
    out[...] = a[...] + b[...]


def add(a, b):
    vmem = pl.BlockSpec(memory_space=pltpu.VMEM)
    return pl.pallas_call(
        add_kernel,
        in_specs=[vmem] * 2,
        out_specs=vmem,
        out_shape=jax.ShapeDtypeStruct(a.shape, a.dtype),
        compiler_params=pltpu.CompilerParams(vmem_limit_bytes=4 * mebibyte),
        name="add",
    )(a, b)


def split_kernel(facts, a, b, keep, send):
    rows = keep.shape[0]
    total = a[...] + b[...]
    kept = facts[fact_kept]
    keep[...] = jnp.where(kept == 0, total[:rows], total[rows:])
    send[...] = jnp.where(kept == 0, total[rows:], total[:rows])


def split(facts, a, b):
    vmem = pl.BlockSpec(memory_space=pltpu.VMEM)
    return pl.pallas_call(
        split_kernel,
        in_specs=[pl.BlockSpec(memory_space=pltpu.SMEM)] + [vmem] * 2,
        out_specs=[vmem] * 2,
        out_shape=[jax.ShapeDtypeStruct((a.shape[0] // 2, a.shape[1]), a.dtype)] * 2,
        compiler_params=pltpu.CompilerParams(vmem_limit_bytes=4 * mebibyte),
        name="split",
    )(facts, a, b)


def finish_kernel(facts, keep, received, ranked, ranked_received, own, other, *refs):
    *outs, factor = refs
    half = own.shape[0]
    core = facts[fact_core]
    for part in range(2):
        base = 2 * half * part
        factor[pl.ds(pl.multiple_of(base + core * half, half), half), :] = own[...]
        factor[pl.ds(pl.multiple_of(base + (1 - core) * half, half), half), :] = other[...]
    scaled = adapter_scale * (ranked[...] + ranked_received[...])
    high = scaled.astype(jnp.bfloat16)
    low = (scaled - high.astype(jnp.float32)).astype(jnp.bfloat16)
    pair = jnp.concatenate([high, low], axis=1)
    added = jnp.dot(pair, factor[...], preferred_element_type=jnp.float32)
    total = (keep[...] + received[...] + added).astype(jnp.bfloat16)
    block = keep.shape[0] // len(outs)
    mine = facts[fact_mine]
    for index in range(len(outs)):
        for offset, out in enumerate(outs):

            @pl.when(mine ^ offset == index)
            def _():
                out[...] = total[index * block : (index + 1) * block].reshape(out.shape)


def finish(facts, keep, received, ranked, ranked_received, own, other, row_count, step_count):
    rows, columns = keep.shape
    pieces = rows // (row_count * step_count)
    vmem = pl.BlockSpec(memory_space=pltpu.VMEM)
    return pl.pallas_call(
        finish_kernel,
        in_specs=[pl.BlockSpec(memory_space=pltpu.SMEM)] + [vmem] * 6,
        out_specs=[vmem] * pieces,
        out_shape=[jax.ShapeDtypeStruct((row_count, step_count, columns), jnp.bfloat16)] * pieces,
        scratch_shapes=[pltpu.VMEM((4 * own.shape[0], columns), jnp.bfloat16)],
        compiler_params=pltpu.CompilerParams(vmem_limit_bytes=16 * mebibyte),
        name="finish",
    )(facts, keep, received, ranked, ranked_received, own, other)


def place_kernel(facts, *refs):
    *pieces, out, sems = refs
    mine = facts[fact_mine]
    copies = []
    for offset, ref in enumerate(pieces):
        width = ref.shape[2]
        columns = pl.ds(pl.multiple_of((mine ^ offset) * width, width), width)
        copies.append(pltpu.make_async_copy(ref, out.at[:, :, columns], sems.at[offset]))
    for copy in copies:
        copy.start()
    for copy in copies:
        copy.wait()


def place(facts, pieces):
    row_count, step_count, width = pieces[0].shape
    anywhere = pl.BlockSpec(memory_space=pl.ANY)
    return pl.pallas_call(
        place_kernel,
        in_specs=[pl.BlockSpec(memory_space=pltpu.SMEM)] + [anywhere] * len(pieces),
        out_specs=anywhere,
        out_shape=jax.ShapeDtypeStruct((row_count, step_count, width * len(pieces)), jnp.bfloat16),
        scratch_shapes=[pltpu.SemaphoreType.DMA((len(pieces),))],
        compiler_params=pltpu.CompilerParams(vmem_limit_bytes=4 * mebibyte),
        name="place",
    )(facts, *pieces)


def shards(
    count,
    queries,
    cache_keys,
    cache_values,
    new_keys,
    new_values,
    cache_lengths,
    base_weight,
    factor_in,
    adapter_output_factor,
):
    order = ring_order(count)
    half = count // 2
    both = ("fsdp", "tp")
    swap = [(0, 1), (1, 0)]
    after = lax.optimization_barrier
    row_count, step_count, head_count, head_width = queries.shape
    slots, key_heads = cache_keys.shape[1:3]
    own_width = factor_in.shape[0]
    width = head_count * head_width // chunk_count
    facts = lax.dynamic_index_in_dim(
        jnp.asarray(facts_table(count, own_width, width)),
        lax.axis_index(both).astype(jnp.int32),
        0,
        keepdims=False,
    )

    own_in, own_out = factor_in.T, adapter_output_factor
    near_in = lax.ppermute(own_in, "fsdp", [(f, f ^ 1) for f in range(count)])
    attended = attend(
        cache_lengths,
        queries,
        cache_keys.reshape(row_count, slots * key_heads, head_width),
        cache_values.reshape(row_count, slots * key_heads, head_width),
        new_keys.reshape(row_count, step_count * key_heads, head_width),
        new_values.reshape(row_count, step_count * key_heads, head_width),
    )
    attended, near_in = after((attended, near_in))
    gathered = [[x] * count for x in attended]
    for step in range(1, half + 1):
        for c, blocks in enumerate(gathered):
            ring_step(blocks, step, order, c)
        if step == 2:
            others = [lax.ppermute(x, "tp", swap) for x in (own_in, near_in, own_out)]
            gathered[0][count - 2], others = after((gathered[0][count - 2], others))
    other_in, other_near_in, other_out = others
    sent = [blocks[i] for blocks in gathered for i in (half - 1, half + 1)]
    ready, token = fetch(base_weight, sent)
    gathered[-1][half], token = after((gathered[-1][half], token))

    ranked = rank_part(facts, token, gathered, (own_in, near_in, other_in, other_near_in))
    features = base_weight.shape[0]
    parts = [(0, features // 2), (features // 2, features)]
    state = None

    def next_part():
        start, stop = parts.pop(0)
        ahead = (parts[0][1] - parts[0][0]) * ahead_share // 16 if parts else 0
        return project(facts, gathered, start, stop, ahead, ready, base_weight, state)

    bit = 2
    while bit < half:
        pairs = [(2 * f + f // half, 2 * (f ^ bit) + f // half) for f in range(count)]
        received = lax.ppermute(ranked, both, pairs)
        if bit == 2:
            received, (state, ready) = after((received, next_part()))
        ranked = add(ranked, received)
        bit *= 2
    pairs = [(2 * f + f // half, 2 * (f ^ half) + f // half) for f in range(count)]
    received = lax.ppermute(ranked, both, pairs)
    if len(parts) > 1:
        received, (state, ready) = after((received, next_part()))
    received, (keep, send) = after((received, next_part()))
    ranked_keep, ranked_send = split(facts, ranked, received)
    ranked_received = lax.ppermute(ranked_send, "tp", swap)
    received = lax.ppermute(send, "tp", swap)
    pieces = finish(
        facts, keep, received, ranked_keep, ranked_received, own_out, other_out, row_count, step_count
    )
    landed = []
    for offset, piece in enumerate(pieces):
        pairs = [
            (2 * f + t, 2 * (f ^ (t * half + offset)) + f // half)
            for f in range(count)
            for t in range(2)
        ]
        landed.append(lax.ppermute(piece, both, pairs))
    return place(facts, landed)


def solution(mesh):
    return jax.shard_map(
        functools.partial(shards, mesh.shape["fsdp"]),
        mesh=mesh,
        in_specs=(
            P(("groups", "fsdp"), None, "tp", None),
            P(("groups", "fsdp"), None, "tp", None),
            P(("groups", "fsdp"), None, "tp", None),
            P(("groups", "fsdp"), None, "tp", None),
            P(("groups", "fsdp"), None, "tp", None),
            P(("groups", "fsdp")),
            P("tp", "fsdp"),
            P(("groups", "fsdp"), "tp"),
            P(("groups", "tp"), "fsdp"),
        ),
        out_specs=P(("groups", "fsdp"), None, "tp"),
        check_vma=False,
    )
```

```python
import functools
import math

import jax
import jax.numpy as jnp
import numpy as np
from jax import lax
from jax.experimental import pallas as pl
from jax.experimental.pallas import tpu as pltpu
from jax.sharding import PartitionSpec as P

adapter_scale = 2.0
chunk_count = 2
fetched = 64
ahead_share = 5
staged_rows = 4
tile_rows = 512
mebibyte = 1024 * 1024


def attend_kernel(
    lengths, queries, keys, values, fresh_keys, fresh_values, *refs
):
    outs, refs = refs[:chunk_count], refs[chunk_count:]
    query_held, key_held, value_held, fresh_key_held, fresh_value_held, key_wide, value_wide, gathered, sems = refs
    row_count, step_count, heads, head_width = query_held.shape
    old_rows, new_rows = key_held.shape[1], fresh_key_held.shape[1]
    groups = new_rows // step_count
    per_group = heads // groups
    slots = old_rows // groups
    columns = key_wide.shape[1] // groups
    rows = step_count * per_group
    exponent_scale = math.log2(math.e) / math.sqrt(head_width)

    fresh = [
        pltpu.make_async_copy(fresh_keys, fresh_key_held, sems.at[0]),
        pltpu.make_async_copy(queries, query_held, sems.at[1]),
        pltpu.make_async_copy(fresh_values, fresh_value_held, sems.at[2]),
    ]
    old_keys = [
        pltpu.make_async_copy(keys.at[row], key_held.at[row], sems.at[3 + row])
        for row in range(row_count)
    ]
    old_values = [
        pltpu.make_async_copy(values.at[row], value_held.at[row], sems.at[3 + row_count + row])
        for row in range(row_count)
    ]
    for copy in fresh:
        copy.start()
    for row in range(min(staged_rows, row_count)):
        old_keys[row].start()
        old_values[row].start()
    for copy in fresh:
        copy.wait()

    column = lax.broadcasted_iota(jnp.int32, (step_count, 1, columns), 2)
    step = lax.broadcasted_iota(jnp.int32, (step_count, 1, columns), 0)
    fresh_seen = (column >= slots) & (column - slots <= step)

    def widen(old, new, wide):
        wide[:old_rows] = old.astype(jnp.float32)
        wide[old_rows : old_rows + new_rows] = new.astype(jnp.float32)
        wide[old_rows + new_rows :] = jnp.zeros_like(wide[old_rows + new_rows :])

    def picked(group):
        return pl.ds(group, columns, stride=groups)

    for row in range(row_count):
        old_keys[row].wait()
        widen(key_held[row], fresh_key_held[row], key_wide.at[row])
        bias = jnp.where((column < jnp.minimum(lengths[row], slots)) | fresh_seen, 0.0, -jnp.inf)
        scores = [
            lax.dot_general(
                query_held[row, :, group * per_group : (group + 1) * per_group, :].reshape(
                    rows, head_width
                ),
                key_wide[row, picked(group), :].astype(jnp.bfloat16),
                (((1,), (1,)), ((), ())),
                preferred_element_type=jnp.float32,
            ).reshape(step_count, per_group, columns)
            + bias
            for group in range(groups)
        ]
        old_values[row].wait()
        if row + staged_rows < row_count:
            old_keys[row + staged_rows].start()
            old_values[row + staged_rows].start()
        widen(value_held[row], fresh_value_held[row], value_wide.at[row])
        tops = [score.max(-1, keepdims=True) for score in scores]
        scores = [
            jnp.exp2((score - top) * exponent_scale) for score, top in zip(scores, tops)
        ]
        totals = [score.sum(-1, keepdims=True) for score in scores]
        weighted = [
            jnp.dot(
                score.astype(jnp.bfloat16).reshape(rows, columns),
                value_wide[row, picked(group), :].astype(jnp.bfloat16),
                preferred_element_type=jnp.float32,
            ).reshape(step_count, per_group, head_width)
            for group, score in enumerate(scores)
        ]
        for group in range(groups):
            result = weighted[group] / totals[group]
            for s in range(step_count):
                place = (row * step_count + s) * heads + group * per_group
                gathered[place : place + per_group, :] = result[s]
    each = heads // chunk_count
    for head in range(heads):
        place = head % each * head_width
        outs[head // each][:, place : place + head_width] = gathered[
            pl.ds(head, row_count * step_count, stride=heads), :
        ].astype(jnp.bfloat16)


def attend(lengths, queries, keys, values, fresh_keys, fresh_values):
    row_count, step_count, heads, head_width = queries.shape
    smem = pl.BlockSpec(memory_space=pltpu.SMEM)
    vmem = pl.BlockSpec(memory_space=pltpu.VMEM)
    anywhere = pl.BlockSpec(memory_space=pl.ANY)
    kind = jnp.bfloat16
    shape = (row_count * step_count, heads * head_width // chunk_count)
    groups = fresh_keys.shape[1] // step_count
    columns = -(-(keys.shape[1] + fresh_keys.shape[1]) // (16 * groups)) * 16
    wide = pltpu.VMEM((row_count, columns * groups, head_width), jnp.float32)
    return pl.pallas_call(
        attend_kernel,
        in_specs=[smem] + [anywhere] * 5,
        out_specs=[vmem] * chunk_count,
        out_shape=[jax.ShapeDtypeStruct(shape, kind)] * chunk_count,
        scratch_shapes=[
            pltpu.VMEM(queries.shape, kind),
            pltpu.VMEM(keys.shape, kind),
            pltpu.VMEM(values.shape, kind),
            pltpu.VMEM(fresh_keys.shape, kind),
            pltpu.VMEM(fresh_values.shape, kind),
            wide,
            wide,
            pltpu.VMEM((row_count * step_count * heads, head_width), jnp.float32),
            pltpu.SemaphoreType.DMA((3 + 2 * row_count,)),
        ],
        compiler_params=pltpu.CompilerParams(vmem_limit_bytes=58 * mebibyte),
        cost_estimate=pl.CostEstimate(
            flops=4 * row_count * step_count * heads * keys.shape[1] * head_width,
            bytes_accessed=4 * keys.size,
            transcendentals=row_count * step_count * heads * keys.shape[1],
        ),
        name="attend",
    )(lengths, queries, keys, values, fresh_keys, fresh_values)


def ring_order(count):
    inner = max(d for d in range(1, count + 1) if count % d == 0 and d * d <= count)
    outer = count // inner
    if inner == 1:
        return list(range(count))
    order = [z * inner for z in range(outer)]
    for turn, z in enumerate(reversed(range(outer))):
        columns = list(range(1, inner))
        if turn % 2:
            columns.reverse()
        order += [z * inner + c for c in columns]
    return order


def ring_step(blocks, step, order, chunk):
    count = len(order)
    up = [(order[i], order[(i + 1) % count]) for i in range(count)]
    down = [(b, a) for a, b in up]
    if step < count // 2 or chunk % 2 == 0:
        blocks[count - step] = lax.ppermute(blocks[(1 - step) % count], "fsdp", up)
    if step < count // 2 or chunk % 2 == 1:
        blocks[step] = lax.ppermute(blocks[step - 1], "fsdp", down)


def output_step(count, core, offset):
    half = count // 2
    return offset ^ ((core ^ (1 if offset >= max(half // 2, 1) else 0)) * half)


def row_slot(count, chip):
    half = count // 2
    mine = chip % half
    return ((chip // half) ^ (1 if mine >= max(half // 2, 1) else 0)) * half + mine


def facts_table(count, own_width, width):
    order = ring_order(count)
    position = {f: i for i, f in enumerate(order)}
    half = count // 2
    rows = []
    for chip in range(count):
        for core in range(2):
            side, mine = chip // half, chip % half
            start = mine // 2 * 2 * own_width
            owner = start // width if core == side else -1
            places = [row_slot(count, order[(position[chip] + i) % count]) for i in range(count)]
            kept = core ^ (row_slot(count, chip) // half)
            rows.append([core, kept, mine, owner, start % width, chip % 2] + places)
    return np.array(rows, np.int32)


fact_core, fact_kept, fact_mine, fact_owner, fact_start, fact_odd, fact_places = range(7)


def collect(facts, blocks, held, columns, sem):
    own = pltpu.make_async_copy(blocks[0].at[:, columns], held.at[facts[fact_places]], sem)
    own.start()
    for offset, ref in enumerate(blocks[1:]):
        held[facts[fact_places + 1 + offset]] = ref[:, columns]
    own.wait()


def block_specs(count):
    vmem = pl.BlockSpec(memory_space=pltpu.VMEM)
    return [pl.BlockSpec(memory_space=pl.ANY)] + [vmem] * (count - 1)


def fetch_kernel(weight, *refs):
    out, token, sem = refs[-3:]
    copy = pltpu.make_async_copy(weight.at[pl.ds(0, out.shape[0]), :], out, sem)
    copy.start()
    token[...] = jnp.zeros_like(token)
    copy.wait()


def fetch(base_weight, after):
    rows, columns = base_weight.shape
    vmem = pl.BlockSpec(memory_space=pltpu.VMEM)
    rows = rows * fetched // 256
    return pl.pallas_call(
        fetch_kernel,
        in_specs=[pl.BlockSpec(memory_space=pl.ANY)] * (1 + len(after)),
        out_specs=[vmem] * 2,
        out_shape=[
            jax.ShapeDtypeStruct((rows, columns), base_weight.dtype),
            jax.ShapeDtypeStruct((8, 128), jnp.float32),
        ],
        scratch_shapes=[pltpu.SemaphoreType.DMA(())],
        compiler_params=pltpu.CompilerParams(vmem_limit_bytes=24 * mebibyte),
        cost_estimate=pl.CostEstimate(flops=0, bytes_accessed=4 * rows * columns, transcendentals=0),
        name="fetch",
    )(base_weight, *after)


def rank_kernel(count, facts, _, *refs):
    chunks, refs = refs[: chunk_count * count], refs[chunk_count * count :]
    factors, (ranked, held, factor, sem) = refs[:4], refs[4:]
    width = held.shape[2]
    half, each = factors[0].shape
    ranked[...] = jnp.zeros_like(ranked)
    for chunk in range(chunk_count):
        blocks = chunks[chunk * count : (chunk + 1) * count]

        @pl.when(facts[fact_owner] == chunk)
        def _():
            start = pl.multiple_of(facts[fact_start], 128)
            collect(facts, blocks, held, pl.ds(start, width), sem)
            core, odd = facts[fact_core], facts[fact_odd]
            for index, ref in enumerate(factors):
                row = core ^ (index // 2)
                column = odd ^ (index % 2)
                factor[
                    pl.ds(pl.multiple_of(row * half, half), half),
                    pl.ds(pl.multiple_of(column * each, each), each),
                ] = ref[...]
            ranked[...] = lax.dot_general(
                held[...].reshape(-1, width),
                factor[...],
                (((1,), (1,)), ((), ())),
                preferred_element_type=jnp.float32,
            )


def rank_part(facts, token, gathered, factors):
    blocks = [x for chunk in gathered for x in chunk]
    count = len(gathered[0])
    block_rows = blocks[0].shape[0]
    half, each = factors[0].shape
    vmem = pl.BlockSpec(memory_space=pltpu.VMEM)
    return pl.pallas_call(
        functools.partial(rank_kernel, count),
        in_specs=[pl.BlockSpec(memory_space=pltpu.SMEM), pl.BlockSpec(memory_space=pl.ANY)]
        + block_specs(count) * chunk_count
        + [vmem] * 4,
        out_specs=vmem,
        out_shape=jax.ShapeDtypeStruct((count * block_rows, 2 * half), jnp.float32),
        scratch_shapes=[
            pltpu.VMEM((count, block_rows, 2 * each), jnp.bfloat16),
            pltpu.VMEM((2 * half, 2 * each), jnp.bfloat16),
            pltpu.SemaphoreType.DMA(()),
        ],
        compiler_params=pltpu.CompilerParams(vmem_limit_bytes=47 * mebibyte),
        cost_estimate=pl.CostEstimate(
            flops=8 * count * block_rows * half * each, bytes_accessed=mebibyte, transcendentals=0
        ),
        name="rank_part",
    )(facts, token, *blocks, *factors)


def project_kernel(start, stop, first, ahead, last, facts, *refs):
    refs = list(refs)
    held, streamed, sem, sems, ahead_sem = refs[-5:]
    count = held.shape[0]
    blocks, refs = refs[:count], refs[count:-5]
    ready, weight, refs = refs[0], refs[1], refs[2:]
    previous = refs.pop(0) if first else None
    width = stop - start
    rows = count * held.shape[1]
    skipped = ready.shape[0]
    edges = [*range(skipped, width, tile_rows), width]
    copies = [
        pltpu.make_async_copy(
            weight.at[pl.ds(first + begin, end - begin), :],
            streamed.at[pl.ds(begin - skipped, end - begin), :],
            sems.at[i],
        )
        for i, (begin, end) in enumerate(zip(edges, edges[1:]))
    ]
    for copy in copies:
        copy.start()
    if ahead:
        later = pltpu.make_async_copy(weight.at[pl.ds(first + width, ahead), :], refs[1], ahead_sem)
        later.start()
    collect(facts, blocks, held, slice(start, stop), sem)

    def product(begin, end, factor):
        return jnp.dot(
            held[:, :, begin:end].reshape(rows, end - begin),
            factor,
            preferred_element_type=jnp.float32,
        )

    total = product(0, skipped, ready[...])
    if first:
        total += previous[...]
    for copy, begin, end in zip(copies, edges, edges[1:]):
        copy.wait()
        total += product(begin, end, streamed[begin - skipped : end - skipped, :])
    if not last:
        refs[0][...] = total
        later.wait()
        return
    keep, send = refs
    kept = facts[fact_kept]
    top, bottom = total[: rows // 2], total[rows // 2 :]
    keep[...] = jnp.where(kept == 0, top, bottom)
    send[...] = jnp.where(kept == 0, bottom, top)


def project(facts, gathered, start, stop, ahead, ready, base_weight, previous):
    features, columns = base_weight.shape
    chunk_width = features // chunk_count
    chunk, start = divmod(start, chunk_width)
    stop = stop - chunk * chunk_width
    first = chunk * chunk_width + start
    blocks = gathered[chunk]
    count = len(blocks)
    block_rows = blocks[0].shape[0]
    rows = count * block_rows
    last = not ahead
    vmem = pl.BlockSpec(memory_space=pltpu.VMEM)
    shape = jax.ShapeDtypeStruct((rows // (1 + last), columns), jnp.float32)
    shapes = [shape] * 2 if last else [shape, jax.ShapeDtypeStruct((ahead, columns), jnp.bfloat16)]
    return pl.pallas_call(
        functools.partial(project_kernel, start, stop, first, ahead, last),
        in_specs=[pl.BlockSpec(memory_space=pltpu.SMEM)]
        + block_specs(count)
        + [vmem, pl.BlockSpec(memory_space=pl.ANY)]
        + [vmem] * (first > 0),
        out_specs=[vmem] * 2,
        out_shape=shapes,
        scratch_shapes=[
            pltpu.VMEM((count, block_rows, stop - start), jnp.bfloat16),
            pltpu.VMEM((stop - start - ready.shape[0], columns), jnp.bfloat16),
            pltpu.SemaphoreType.DMA(()),
            pltpu.SemaphoreType.DMA((-(-(stop - start - ready.shape[0]) // tile_rows),)),
            pltpu.SemaphoreType.DMA(()),
        ],
        compiler_params=pltpu.CompilerParams(vmem_limit_bytes=26 * mebibyte),
        cost_estimate=pl.CostEstimate(
            flops=2 * rows * (stop - start) * columns,
            bytes_accessed=2 * (stop - start) * columns,
            transcendentals=0,
        ),
        name=f"project_{first}",
    )(facts, *blocks, ready, base_weight, *([previous] if first else []))


def add_kernel(a, b, out):
    out[...] = a[...] + b[...]


def add(a, b):
    vmem = pl.BlockSpec(memory_space=pltpu.VMEM)
    return pl.pallas_call(
        add_kernel,
        in_specs=[vmem] * 2,
        out_specs=vmem,
        out_shape=jax.ShapeDtypeStruct(a.shape, a.dtype),
        compiler_params=pltpu.CompilerParams(vmem_limit_bytes=4 * mebibyte),
        name="add",
    )(a, b)


def split_kernel(facts, a, b, keep, send):
    rows = keep.shape[0]
    total = a[...] + b[...]
    kept = facts[fact_kept]
    keep[...] = jnp.where(kept == 0, total[:rows], total[rows:])
    send[...] = jnp.where(kept == 0, total[rows:], total[:rows])


def split(facts, a, b):
    vmem = pl.BlockSpec(memory_space=pltpu.VMEM)
    return pl.pallas_call(
        split_kernel,
        in_specs=[pl.BlockSpec(memory_space=pltpu.SMEM)] + [vmem] * 2,
        out_specs=[vmem] * 2,
        out_shape=[jax.ShapeDtypeStruct((a.shape[0] // 2, a.shape[1]), a.dtype)] * 2,
        compiler_params=pltpu.CompilerParams(vmem_limit_bytes=4 * mebibyte),
        name="split",
    )(facts, a, b)


def finish_kernel(facts, keep, received, ranked, ranked_received, own, other, *refs):
    *outs, factor = refs
    half = own.shape[0]
    core = facts[fact_core]
    for part in range(2):
        base = 2 * half * part
        factor[pl.ds(pl.multiple_of(base + core * half, half), half), :] = own[...]
        factor[pl.ds(pl.multiple_of(base + (1 - core) * half, half), half), :] = other[...]
    scaled = adapter_scale * (ranked[...] + ranked_received[...])
    high = scaled.astype(jnp.bfloat16)
    low = (scaled - high.astype(jnp.float32)).astype(jnp.bfloat16)
    pair = jnp.concatenate([high, low], axis=1)
    added = jnp.dot(pair, factor[...], preferred_element_type=jnp.float32)
    total = (keep[...] + received[...] + added).astype(jnp.bfloat16)
    block = keep.shape[0] // len(outs)
    mine = facts[fact_mine]
    for index in range(len(outs)):
        for offset, out in enumerate(outs):

            @pl.when(mine ^ offset == index)
            def _():
                out[...] = total[index * block : (index + 1) * block].reshape(out.shape)


def finish(facts, keep, received, ranked, ranked_received, own, other, row_count, step_count):
    rows, columns = keep.shape
    pieces = rows // (row_count * step_count)
    vmem = pl.BlockSpec(memory_space=pltpu.VMEM)
    return pl.pallas_call(
        finish_kernel,
        in_specs=[pl.BlockSpec(memory_space=pltpu.SMEM)] + [vmem] * 6,
        out_specs=[vmem] * pieces,
        out_shape=[jax.ShapeDtypeStruct((row_count, step_count, columns), jnp.bfloat16)] * pieces,
        scratch_shapes=[pltpu.VMEM((4 * own.shape[0], columns), jnp.bfloat16)],
        compiler_params=pltpu.CompilerParams(vmem_limit_bytes=16 * mebibyte),
        name="finish",
    )(facts, keep, received, ranked, ranked_received, own, other)


def place_kernel(facts, *refs):
    *pieces, out, sems = refs
    mine = facts[fact_mine]
    copies = []
    for offset, ref in enumerate(pieces):
        width = ref.shape[2]
        columns = pl.ds(pl.multiple_of((mine ^ offset) * width, width), width)
        copies.append(pltpu.make_async_copy(ref, out.at[:, :, columns], sems.at[offset]))
    for copy in copies:
        copy.start()
    for copy in copies:
        copy.wait()


def place(facts, pieces):
    row_count, step_count, width = pieces[0].shape
    anywhere = pl.BlockSpec(memory_space=pl.ANY)
    return pl.pallas_call(
        place_kernel,
        in_specs=[pl.BlockSpec(memory_space=pltpu.SMEM)] + [anywhere] * len(pieces),
        out_specs=anywhere,
        out_shape=jax.ShapeDtypeStruct((row_count, step_count, width * len(pieces)), jnp.bfloat16),
        scratch_shapes=[pltpu.SemaphoreType.DMA((len(pieces),))],
        compiler_params=pltpu.CompilerParams(vmem_limit_bytes=4 * mebibyte),
        name="place",
    )(facts, *pieces)


def shards(
    count,
    queries,
    cache_keys,
    cache_values,
    new_keys,
    new_values,
    cache_lengths,
    base_weight,
    factor_in,
    adapter_output_factor,
):
    order = ring_order(count)
    half = count // 2
    both = ("fsdp", "tp")
    swap = [(0, 1), (1, 0)]
    after = lax.optimization_barrier
    row_count, step_count, head_count, head_width = queries.shape
    slots, key_heads = cache_keys.shape[1:3]
    own_width = factor_in.shape[0]
    width = head_count * head_width // chunk_count
    facts = lax.dynamic_index_in_dim(
        jnp.asarray(facts_table(count, own_width, width)),
        lax.axis_index(both).astype(jnp.int32),
        0,
        keepdims=False,
    )

    own_in, own_out = factor_in.T, adapter_output_factor
    near_in = lax.ppermute(own_in, "fsdp", [(f, f ^ 1) for f in range(count)])
    attended = attend(
        cache_lengths,
        queries,
        cache_keys.reshape(row_count, slots * key_heads, head_width),
        cache_values.reshape(row_count, slots * key_heads, head_width),
        new_keys.reshape(row_count, step_count * key_heads, head_width),
        new_values.reshape(row_count, step_count * key_heads, head_width),
    )
    attended, near_in = after((attended, near_in))
    gathered = [[x] * count for x in attended]
    for step in range(1, half + 1):
        for c, blocks in enumerate(gathered):
            ring_step(blocks, step, order, c)
        if step == 2:
            others = [lax.ppermute(x, "tp", swap) for x in (own_in, near_in, own_out)]
            gathered[0][count - 2], others = after((gathered[0][count - 2], others))
    other_in, other_near_in, other_out = others
    sent = [blocks[i] for blocks in gathered for i in (half - 1, half + 1)]
    ready, token = fetch(base_weight, sent)
    gathered[-1][half], token = after((gathered[-1][half], token))

    ranked = rank_part(facts, token, gathered, (own_in, near_in, other_in, other_near_in))
    features = base_weight.shape[0]
    parts = [(0, features // 2), (features // 2, features)]
    state = None

    def next_part():
        start, stop = parts.pop(0)
        ahead = (parts[0][1] - parts[0][0]) * ahead_share // 16 if parts else 0
        return project(facts, gathered, start, stop, ahead, ready, base_weight, state)

    bit = 2
    while bit < half:
        pairs = [(2 * f + f // half, 2 * (f ^ bit) + f // half) for f in range(count)]
        received = lax.ppermute(ranked, both, pairs)
        if bit == 2:
            received, (state, ready) = after((received, next_part()))
        ranked = add(ranked, received)
        bit *= 2
    pairs = [(2 * f + f // half, 2 * (f ^ half) + f // half) for f in range(count)]
    received = lax.ppermute(ranked, both, pairs)
    if len(parts) > 1:
        received, (state, ready) = after((received, next_part()))
    received, (keep, send) = after((received, next_part()))
    ranked_keep, ranked_send = split(facts, ranked, received)
    ranked_received = lax.ppermute(ranked_send, "tp", swap)
    received = lax.ppermute(send, "tp", swap)
    pieces = finish(
        facts, keep, received, ranked_keep, ranked_received, own_out, other_out, row_count, step_count
    )
    landed = []
    for offset, piece in enumerate(pieces):
        pairs = [
            (2 * f + t, 2 * (f ^ output_step(count, t, offset)) + f // half)
            for f in range(count)
            for t in range(2)
        ]
        landed.append(lax.ppermute(piece, both, pairs))
    return place(facts, landed)


def solution(mesh):
    return jax.shard_map(
        functools.partial(shards, mesh.shape["fsdp"]),
        mesh=mesh,
        in_specs=(
            P(("groups", "fsdp"), None, "tp", None),
            P(("groups", "fsdp"), None, "tp", None),
            P(("groups", "fsdp"), None, "tp", None),
            P(("groups", "fsdp"), None, "tp", None),
            P(("groups", "fsdp"), None, "tp", None),
            P(("groups", "fsdp")),
            P("tp", "fsdp"),
            P(("groups", "fsdp"), "tp"),
            P(("groups", "tp"), "fsdp"),
        ),
        out_specs=P(("groups", "fsdp"), None, "tp"),
        check_vma=False,
    )
```
